32 devices in a mesh: gx: 4 (over z), gy: 4 (over y, x), gz: 2 (over core).
Axes of the slice: x: 2, y: 2, z: 4, core: 2. Of those that a mesh axis runs over, the one named last changes fastest.
Arguments:
- e_field: float32 [3, 64, 32, 1024], P(None, 'gx', 'gz', 'gy'), may hold values from -6 to 6
- h_field: float32 [3, 64, 32, 1024], P(None, 'gx', 'gz', 'gy'), may hold values from -6 to 6
- polar: float32 [3, 64, 32, 1024], P(None, 'gx', 'gz', 'gy'), may hold values from -4 to 4
- permittivity: float32 [64, 32, 1024], P('gx', 'gz', 'gy'), may hold values from 1 to 4
- resonance: float32 [64, 32, 1024], P('gx', 'gz', 'gy'), may hold values from 0.3 to 1.2
- dispersive: int32 [64, 32, 8], P('gx', 'gz', 'gy'), may hold values 0 or 1
Outputs:
- e_final: float32 [3, 64, 32, 1024], P(None, 'gx', 'gz', 'gy')
- h_final: float32 [3, 64, 32, 1024], P(None, 'gx', 'gz', 'gy')
The draws below stay inside these ranges and needn't reach their ends.
All inputs are finite; a program needn't handle non-finite values. No bound on the sum of `dispersive` on one device may be relied on, other than what follows from the above.
Results may differ from the reference program's by a relative error of at most 0.00002.
Values sent between devices are 32-bit elements; how exact they have to be, the bound alone decides.
No kernel may reach another device: no remote copies, remote signals or barrier semaphores. Data moves between devices by JAX's collectives and lax.ppermute only.
A program may use at most 64 MiB of HBM per device.

```python
import math
import jax
import jax.numpy as jnp
from jax import lax

STEPS = 5
NPML = 8
NX = 64
NY = 1024
NZ = 32
NBY = 8


def place_ends(entries, rng, least, top_value):
    longest = entries.shape.index(max(entries.shape))
    spots = []
    for shift in (0, 1):
        where = [jax.random.randint(jax.random.fold_in(rng, axis), (), 0, length) for axis, length in enumerate(entries.shape)]
        where[longest] = (where[longest] + shift) % entries.shape[longest]
        spots.append(tuple(where))
    return entries.at[spots[0]].set(least).at[spots[1]].set(top_value)


def level_of(key, dims, pieces, low, top_value):
    loudness, own = 1.0, jax.random.fold_in(key, 6)
    for axis_at, shards_of in pieces:
        heights = jnp.exp(jax.random.uniform(jax.random.fold_in(own, axis_at), (shards_of,), jnp.float32, low / len(pieces), top_value / len(pieces)))
        loudness = loudness * jnp.repeat(heights, dims[axis_at] // shards_of).reshape([-1 if axis == axis_at else 1 for axis in range(len(dims))])
    return loudness


def bell_draw(key, extent, spread, reach, split=(), held_as=jnp.bfloat16):
    array = jax.random.normal(key, extent, jnp.float32) * spread
    if len(split) > 0:
        array = level_of(key, extent, split, -0.22, 0.18) * array
    return jnp.clip(array, min=-reach, max=reach).astype(held_as)


def setup_inputs(seed: int = 0) -> dict:
    arg_keys = jax.random.split(jax.random.key(seed), 7)
    return {
        "e_field": bell_draw(arg_keys[0], (3, NX, NZ, NY), 1.0, 6.0, ((1, 4), (2, 2), (3, 4)), jnp.float32),
        "h_field": bell_draw(arg_keys[1], (3, NX, NZ, NY), 1.0, 6.0, ((1, 4), (2, 2), (3, 4)), jnp.float32),
        "polar": bell_draw(arg_keys[2], (3, NX, NZ, NY), 0.5, 4.0, ((1, 4), (2, 2), (3, 4)), jnp.float32),
        "permittivity": jnp.clip(jnp.exp(math.log(4.0) - 1.3862944 * jax.random.uniform(arg_keys[3], (NX, NZ, NY), jnp.float32) ** level_of(arg_keys[3], (NX, NZ, NY), ((0, 4), (1, 2), (2, 4)), -0.2, 0.2)), 1.0, 4.0),
        "resonance": jnp.clip(jnp.exp(math.log(1.2) - 1.3862944 * jax.random.uniform(arg_keys[4], (NX, NZ, NY), jnp.float32) ** level_of(arg_keys[4], (NX, NZ, NY), ((0, 4), (1, 2), (2, 4)), -0.2, 0.2)), 0.3, 1.2),
        "dispersive": place_ends((jax.random.randint(arg_keys[5], (NX, NZ, NBY), 0, 2) < 1).astype(jnp.int32), jax.random.fold_in(arg_keys[5], 1), 0, 1),
    }


DT = 0.5
DAMPING = 0.1
STRENGTH = 3.0
SMAX = 0.8


def ahead(f, axis):
    size = f.shape[axis]
    return jnp.concatenate([lax.slice_in_dim(f, 1, size, axis=axis), jnp.zeros_like(lax.slice_in_dim(f, 0, 1, axis=axis))], axis=axis)


def behind(f, axis):
    size = f.shape[axis]
    return jnp.concatenate([jnp.zeros_like(lax.slice_in_dim(f, 0, 1, axis=axis)), lax.slice_in_dim(f, 0, size - 1, axis=axis)], axis=axis)


def curl_forward(f):
    xpair = ahead(f[1:3], 1)
    ypair = ahead(jnp.stack([f[0], f[2]]), 3)
    zpair = ahead(f[0:2], 2)
    dxy = xpair[0] - f[1]
    dxz = xpair[1] - f[2]
    dyx = ypair[0] - f[0]
    dyz = ypair[1] - f[2]
    dzx = zpair[0] - f[0]
    dzy = zpair[1] - f[1]
    return jnp.stack([dyz - dzy, dzx - dxz, dxy - dyx])


def curl_backward(f):
    xpair = behind(f[1:3], 1)
    ypair = behind(jnp.stack([f[0], f[2]]), 3)
    zpair = behind(f[0:2], 2)
    dxy = f[1] - xpair[0]
    dxz = f[2] - xpair[1]
    dyx = f[0] - ypair[0]
    dyz = f[2] - ypair[1]
    dzx = f[0] - zpair[0]
    dzy = f[1] - zpair[1]
    return jnp.stack([dyz - dzy, dzx - dxz, dxy - dyx])


def profile(index, total):
    depth = jnp.maximum(NPML - index, 0.0) + jnp.maximum(index - (total - 1 - NPML), 0.0)
    return SMAX * (depth / NPML) ** 3


def reference(e_field, h_field, polar, permittivity, resonance, dispersive):
    xpos = jnp.arange(NX).astype(jnp.float32)
    ypos = jnp.arange(NY).astype(jnp.float32)
    sigma = profile(xpos, NX)[:, None, None] + profile(ypos, NY)[None, None, :]
    half = sigma * DT / 2.0
    h_keep = (1.0 - half) / (1.0 + half)
    h_gain = DT / (1.0 + half)
    e_keep = (permittivity - half) / (permittivity + half)
    e_gain = DT / (permittivity + half)
    wsq = (resonance * DT) ** 2
    denom = 1.0 + DAMPING * DT / 2.0
    coef_one = (2.0 - wsq) / denom
    coef_two = (1.0 - DAMPING * DT / 2.0) / denom
    coef_three = STRENGTH * wsq / denom
    marks = jnp.repeat(dispersive.astype(jnp.float32), 128, axis=2)
    efield, hfield, pnow, pold = e_field, h_field, polar, polar
    for step in range(STEPS):
        hfield = h_keep * hfield - h_gain * curl_forward(efield)
        pnext = marks * (coef_one * pnow - coef_two * pold + coef_three * efield)
        efield = e_keep * efield + e_gain * curl_backward(hfield) - (e_gain / DT) * (pnext - marks * pnow)
        pold = pnow
        pnow = pnext
    return efield, hfield
```

```python
import functools
import jax
import jax.numpy as jnp
from jax import lax
from jax.experimental import pallas as pl
from jax.experimental.pallas import tpu as pltpu
from jax.sharding import PartitionSpec as P

STEPS = 5
NPML = 8
DT = 0.5
DAMPING = 0.1
STRENGTH = 3.0
SMAX = 0.8
DENOM = 1.0 + DAMPING * DT / 2.0
KEEP = (1.0 - DAMPING * DT / 2.0) / DENOM

LANES = 128
ROWS = 8
SLOT = 8
GUARD = 8
VMEM_LIMIT = 56 * 1024 * 1024

EX, HX, PX, EPS, RES = 0, 3, 6, 9, 10
ARRAYS = 11


def faces(count):
    up, down = [], []
    last = count - STEPS
    for c in range(3):
        up.append((EX + c, last, STEPS))
        down.append((EX + c, 0, STEPS if c > 0 else STEPS - 1))
    for c in range(3):
        up.append((HX + c, last if c > 0 else last + 1, STEPS if c > 0 else STEPS - 1))
        down.append((HX + c, 0, STEPS - 1))
    for c in range(3):
        up.append((PX + c, last + 1, STEPS - 1))
        down.append((PX + c, 0, STEPS - 1 if c > 0 else STEPS - 2))
    for a in (EPS, RES):
        up.append((a, last + 1, STEPS - 1))
        down.append((a, 0, STEPS - 1))
    return up, down


def planes_of(parts):
    return sum(count for _, _, count in parts)


def pick(refs, array):
    e_ref, h_ref, p_ref, eps_ref, res_ref = refs
    if array < HX:
        return e_ref.at[array]
    if array < PX:
        return h_ref.at[array - HX]
    if array < EPS:
        return p_ref.at[array - PX]
    return eps_ref if array == EPS else res_ref


def pack_faces(e_ref, h_ref, p_ref, eps_ref, freq_ref, mark_ref, up_ref, down_ref, side_ref, res_ref):
    xcount, zcount, ycount = eps_ref.shape
    core = lax.axis_index("gz")
    for z in range(0, zcount, ROWS):
        for j in range(ycount // LANES):
            lanes = slice(j * LANES, (j + 1) * LANES)
            mark = mark_ref[:, z : z + ROWS, j : j + 1].astype(jnp.float32)
            freq = freq_ref[:, z : z + ROWS, lanes] * DT
            res_ref[:, z : z + ROWS, lanes] = mark * (freq * freq / DENOM)
    refs = (e_ref, h_ref, p_ref, eps_ref, res_ref)
    for parts, out_ref in zip(faces(xcount), (up_ref, down_ref)):
        at = 0
        for array, first, count in parts:
            out_ref[at : at + count] = pick(refs, array)[first : first + count]
            at += count
    begin = pl.multiple_of((1 - core) * (zcount - ROWS), ROWS)
    for array in range(ARRAYS):
        side_ref[array] = pick(refs, array)[:, pl.ds(begin, ROWS), :]


def pack_strips(e_ref, h_ref, p_ref, eps_ref, res_ref, side_ref, low_ref, high_ref):
    xcount, zcount, ycount = eps_ref.shape
    core = lax.axis_index("gz")
    refs = (e_ref, h_ref, p_ref, eps_ref, res_ref)
    own = pl.multiple_of(core * ROWS, ROWS)
    halo = pl.multiple_of((1 - core) * zcount, ROWS)
    slot = lax.broadcasted_iota(jnp.int32, (ROWS, LANES), 1) // SLOT
    for array in range(ARRAYS):
        src = pick(refs, array)
        for z in range(0, zcount + ROWS, ROWS):
            low = high = jnp.zeros((ROWS, LANES), jnp.float32)
            for x in range(xcount):
                if z < zcount:
                    first, last = src[x, z : z + ROWS, 0:LANES], src[x, z : z + ROWS, ycount - LANES : ycount]
                else:
                    first, last = side_ref[array, x, :, 0:LANES], side_ref[array, x, :, ycount - LANES : ycount]
                here = slot == x
                low = jnp.where(here, pltpu.roll(first, SLOT * x, 1) if x else first, low)
                shift = (SLOT * x + SLOT) % LANES
                high = jnp.where(here, pltpu.roll(last, shift, 1) if shift else last, high)
            rows = pl.ds(own + z, ROWS) if z < zcount else pl.ds(halo, ROWS)
            low_ref[array, rows, :] = low
            high_ref[array, rows, :] = high


def pack_corners(ahead_ref, behind_ref, up_ref, down_ref):
    wide = STEPS * SLOT
    lane = lax.broadcasted_iota(jnp.int32, (1, 1, LANES), 2)
    ahead, behind = ahead_ref[...], behind_ref[...]
    up_ref[...] = jnp.where(lane >= LANES - wide, ahead, pltpu.roll(behind, wide, 2))
    down_ref[...] = jnp.where(lane < wide, ahead, pltpu.roll(behind, LANES - wide, 2))


def profile(index, total):
    depth = jnp.maximum(NPML - index, 0.0) + jnp.maximum(index - (total - 1 - NPML), 0.0)
    return SMAX * (depth / NPML) ** 3


def turn(value, shift):
    shift = shift % LANES
    return pltpu.roll(value, shift, 1) if shift else value


def advance(
    e_ref, h_ref, p_ref, eps_ref, res_ref, side_ref, low_ref, low_side_ref, high_ref, high_side_ref,
    ahead_ref, behind_ref, corner_low_ref, corner_high_ref, e_out, h_out,
    E, H, R, U, EC, EB, BM, HC, HB,
):
    xcount, zcount, ycount = eps_ref.shape
    tiles = ycount // LANES
    core = lax.axis_index("gz")
    xplace = lax.axis_index("gx") * xcount
    yplace = lax.axis_index("gy") * ycount
    xtotal = xcount * lax.axis_size("gx")
    ytotal = ycount * lax.axis_size("gy")
    own = pl.multiple_of(GUARD + core * ROWS, ROWS)
    halo = pl.multiple_of(GUARD + (1 - core) * zcount, ROWS)
    near = pl.multiple_of(core * (zcount - ROWS), ROWS)
    zsteps = (zcount + ROWS) // ROWS
    lane = lax.broadcasted_iota(jnp.int32, (ROWS, LANES), 1)
    is_ahead, is_behind = lane < SLOT, lane >= LANES - SLOT
    wide = STEPS * SLOT

    def put(array, plane, row, j, value):
        if array < HX:
            E[array, plane, j, pl.ds(row, ROWS), :] = value
        elif array < PX:
            H[array - HX, plane, j, pl.ds(row, ROWS), :] = value * (1.0 / 6.0)
        elif array < EPS:
            R[array - PX, plane, j, pl.ds(row, ROWS), :] = value * (1.0 / 3.0)
        elif array == EPS:
            EC[plane, j, pl.ds(row, ROWS), :] = value
        else:
            BM[plane, j, pl.ds(row, ROWS), :] = value

    refs = (e_ref, h_ref, p_ref, eps_ref, res_ref)
    for array in range(ARRAYS):
        src = pick(refs, array)

        def own_plane(x, _, array=array, src=src):
            for j in range(tiles):
                lanes = slice(j * LANES, (j + 1) * LANES)
                for z in range(0, zcount, ROWS):
                    put(array, x + STEPS, own + z, j, src[x, z : z + ROWS, lanes])
                put(array, x + STEPS, halo, j, side_ref[array, x, :, lanes])
            return _

        lax.fori_loop(0, xcount, own_plane, 0, unroll=4)
        for x in range(xcount):
            for t in range(zsteps):
                rows = slice(t * ROWS, (t + 1) * ROWS)
                a = turn(ahead_ref[array, rows, :], -SLOT * x)
                b = turn(behind_ref[array, rows, :], LANES - SLOT - SLOT * x)
                put(array, x + STEPS, GUARD + t * ROWS, tiles, jnp.where(is_ahead, a, jnp.where(is_behind, b, 0.0)))
    ups, downs = faces(xcount)
    for parts, face, face_side, corner, above in (
        (ups, low_ref, low_side_ref, corner_low_ref, False),
        (downs, high_ref, high_side_ref, corner_high_ref, True),
    ):
        at = 0
        for array, first, count in parts:
            base = xcount + STEPS if above else first + STEPS - xcount
            for i in range(count):
                plane = base + i
                for j in range(tiles):
                    lanes = slice(j * LANES, (j + 1) * LANES)
                    for z in range(0, zcount, ROWS):
                        put(array, plane, own + z, j, face[at + i, z : z + ROWS, lanes])
                    put(array, plane, halo, j, face_side[at + i, pl.ds(near, ROWS), lanes])
                slot = plane - (xcount + STEPS) if above else plane
                for t in range(zsteps):
                    rows = slice(t * ROWS, (t + 1) * ROWS)
                    c = corner[array, rows, :]
                    if above:
                        a, b = turn(c, -SLOT * slot), turn(c, (LANES - SLOT) - (LANES - wide + SLOT * slot))
                    else:
                        a, b = turn(c, -(LANES - wide + SLOT * slot)), turn(c, (LANES - SLOT) - SLOT * slot)
                    put(array, plane, GUARD + t * ROWS, tiles, jnp.where(is_ahead, a, jnp.where(is_behind, b, 0.0)))
            at += count
    extent = xcount + 2 * STEPS
    for j in range(tiles + 1):
        for t in range(zsteps):
            rows = pl.ds(GUARD + t * ROWS, ROWS)
            H[0, 0, j, rows, :] = jnp.zeros((ROWS, LANES), jnp.float32)
            E[0, extent - 1, j, rows, :] = jnp.zeros((ROWS, LANES), jnp.float32)
            R[0, extent - 2, j, rows, :] = jnp.zeros((ROWS, LANES), jnp.float32)

    def guards(x, _):
        for j in range(tiles + 1):
            for c in range(3):
                H[c, x, j, 0:GUARD, :] = jnp.zeros((ROWS, LANES), jnp.float32)
                E[c, x, j, GUARD + zcount + ROWS : GUARD + zcount + 2 * ROWS, :] = jnp.zeros((ROWS, LANES), jnp.float32)
        return _

    lax.fori_loop(0, extent, guards, 0)

    def coefficients(x, _):
        xpos = xplace + x - STEPS
        xin = (xpos >= 0) & (xpos < xtotal)
        xsigma = profile(jnp.full((ROWS, LANES), xpos, jnp.int32).astype(jnp.float32), xtotal)
        for j in range(tiles + 1):
            if j < tiles:
                ypos = yplace + j * LANES + lane
                inside = jnp.full((ROWS, LANES), xin)
            else:
                ypos = yplace + jnp.where(lane < SLOT, ycount + lane, lane - LANES)
                inside = (is_ahead | is_behind) & (ypos >= 0) & (ypos < ytotal) & xin
            half = (xsigma + profile(ypos.astype(jnp.float32), ytotal)) * (DT / 2.0)
            over = 1.0 / (1.0 + half)
            HC[x, j] = jnp.where(inside, (1.0 - half) * over, 0.0)
            HB[x, j] = jnp.where(inside, (DT / 6.0) * over, 0.0)
            for t in range(zsteps):
                rows = pl.ds(GUARD + t * ROWS, ROWS)
                eps = EC[x, j, rows, :]
                over = 1.0 / jnp.where(inside, eps + half, 1.0)
                EC[x, j, rows, :] = jnp.where(inside, (eps - half) * over, 0.0)
                EB[x, j, rows, :] = jnp.where(inside, (6.0 * DT) * over, 0.0)
        return _

    lax.fori_loop(1, extent - 1, coefficients, 0)
    xpos = xplace - STEPS
    xsigma = profile(jnp.full((ROWS, LANES), xpos, jnp.int32).astype(jnp.float32), xtotal)
    for j in range(tiles + 1):
        if j < tiles:
            ypos = yplace + j * LANES + lane
            inside = jnp.full((ROWS, LANES), xpos >= 0)
        else:
            ypos = yplace + jnp.where(lane < SLOT, ycount + lane, lane - LANES)
            inside = (is_ahead | is_behind) & (ypos >= 0) & (ypos < ytotal) & (xpos >= 0)
        half = (xsigma + profile(ypos.astype(jnp.float32), ytotal)) * (DT / 2.0)
        over = 1.0 / (1.0 + half)
        HC[0, j] = jnp.where(inside, (1.0 - half) * over, 0.0)
        HB[0, j] = jnp.where(inside, (DT / 6.0) * over, 0.0)

    last_lane, first_lane = lane == LANES - 1, lane == 0

    def next_lane(v):
        r = [pltpu.roll(t, LANES - 1, 1) for t in v]
        return [jnp.where(last_lane, r[(j + 1) % len(v)], r[j]) for j in range(len(v))]

    def previous_lane(v):
        r = [pltpu.roll(t, 1, 1) for t in v]
        return [jnp.where(first_lane, r[j - 1], r[j]) for j in range(len(v))]

    def load(ref, c, x, row):
        return [ref[c, x, j, pl.ds(row, ROWS), :] for j in range(tiles + 1)]

    def magnetic(x):
        for t in range(zsteps):
            row = GUARD + t * ROWS
            ex, ey, ez = (load(E, c, x, row) for c in range(3))
            ex_z, ey_z = (load(E, c, x, row + 1) for c in (0, 1))
            ey_x, ez_x = (load(E, c, x + 1, row) for c in (1, 2))
            ex_y, ez_y = next_lane(ex), next_lane(ez)
            for j in range(tiles + 1):
                hc, hb = HC[x, j], HB[x, j]
                rows = pl.ds(row, ROWS)
                H[0, x, j, rows, :] = hc * H[0, x, j, rows, :] - hb * ((ez_y[j] - ez[j]) - (ey_z[j] - ey[j]))
                H[1, x, j, rows, :] = hc * H[1, x, j, rows, :] - hb * ((ex_z[j] - ex[j]) - (ez_x[j] - ez[j]))
                H[2, x, j, rows, :] = hc * H[2, x, j, rows, :] - hb * ((ey_x[j] - ey[j]) - (ex_y[j] - ex[j]))

    def electric(x, first):
        for t in range(zsteps):
            row = GUARD + t * ROWS
            hx, hy, hz = (load(H, c, x, row) for c in range(3))
            hx_z, hy_z = (load(H, c, x, row - 1) for c in (0, 1))
            hy_x, hz_x = (load(H, c, x - 1, row) for c in (1, 2))
            hx_y, hz_y = previous_lane(hx), previous_lane(hz)
            for j in range(tiles + 1):
                rows = pl.ds(row, ROWS)
                ec, eb, bm = EC[x, j, rows, :], EB[x, j, rows, :], BM[x, j, rows, :]
                curls = (
                    (hz[j] - hz_y[j]) - (hy[j] - hy_z[j]),
                    (hx[j] - hx_z[j]) - (hz[j] - hz_x[j]),
                    (hy[j] - hy_x[j]) - (hx[j] - hx_y[j]),
                )
                for c in range(3):
                    e, r = E[c, x, j, rows, :], R[c, x, j, rows, :]
                    u = bm * (e - r)
                    if not first:
                        u = KEEP * U[c, x, j, rows, :] + u
                    U[c, x, j, rows, :] = u
                    R[c, x, j, rows, :] = r + u
                    E[c, x, j, rows, :] = ec * e + eb * (curls[c] - u)

    for step in range(1, STEPS + 1):
        reach = STEPS - step

        def sweep_h(x, _):
            magnetic(x)
            return _

        def sweep_e(x, _, first=step == 1):
            electric(x, first)
            return _

        lax.fori_loop(step - 1, STEPS + xcount + reach, sweep_h, 0)
        lax.fori_loop(step, STEPS + xcount + reach, sweep_e, 0)

    def finish(x, _):
        for c in range(3):
            for j in range(tiles):
                lanes = slice(j * LANES, (j + 1) * LANES)
                for z in range(0, zcount, ROWS):
                    e_out[c, x, z : z + ROWS, lanes] = E[c, x + STEPS, j, pl.ds(own + z, ROWS), :]
                    h_out[c, x, z : z + ROWS, lanes] = H[c, x + STEPS, j, pl.ds(own + z, ROWS), :] * 6.0
        return _

    lax.fori_loop(0, xcount, finish, 0)


def call(kernel, outs, args, scratch=()):
    return pl.pallas_call(
        kernel,
        out_shape=[jax.ShapeDtypeStruct(s, jnp.float32) for s in outs],
        in_specs=[pl.BlockSpec(memory_space=pltpu.VMEM)] * len(args),
        out_specs=[pl.BlockSpec(memory_space=pltpu.VMEM)] * len(outs),
        scratch_shapes=[pltpu.VMEM(s, jnp.float32) for s in scratch],
        compiler_params=pltpu.CompilerParams(vmem_limit_bytes=VMEM_LIMIT),
    )(*args)


def shift(value, axis, by):
    count = lax.axis_size(axis)
    return lax.ppermute(value, axis, [(i, i + by) for i in range(count) if 0 <= i + by < count])


def swap(value):
    return lax.ppermute(value, "gz", [(0, 1), (1, 0)])


def body(e_field, h_field, polar, permittivity, resonance, dispersive):
    xcount, zcount, ycount = permittivity.shape
    ups, downs = faces(xcount)
    up, down, side, res = call(
        pack_faces,
        [
            (planes_of(ups), zcount, ycount),
            (planes_of(downs), zcount, ycount),
            (ARRAYS, xcount, ROWS, ycount),
            (xcount, zcount, ycount),
        ],
        (e_field, h_field, polar, permittivity, resonance, dispersive),
    )
    low, high = shift(up, "gx", 1), shift(down, "gx", -1)
    side = swap(side)
    strip = (ARRAYS, zcount + ROWS, LANES)
    first, last = call(pack_strips, [strip, strip], (e_field, h_field, polar, permittivity, res, side))
    ahead, behind = shift(first, "gy", -1), shift(last, "gy", 1)
    corner_up, corner_down = call(pack_corners, [strip, strip], (ahead, behind))
    corner_low, corner_high = shift(corner_up, "gx", 1), shift(corner_down, "gx", -1)
    low_side, high_side = swap(low), swap(high)
    extent, tiles = xcount + 2 * STEPS, ycount // LANES + 1
    rows = zcount + ROWS + 2 * GUARD
    field, plane = (3, extent, tiles, rows, LANES), (extent, tiles, rows, LANES)
    flat = (extent, tiles, ROWS, LANES)
    return tuple(
        call(
            advance,
            [e_field.shape, h_field.shape],
            (
                e_field, h_field, polar, permittivity, res, side, low, low_side, high, high_side,
                ahead, behind, corner_low, corner_high,
            ),
            [field] * 4 + [plane] * 3 + [flat] * 2,
        )
    )


def solution(mesh):
    field, cell = P(None, "gx", "gz", "gy"), P("gx", "gz", "gy")
    return jax.shard_map(
        body,
        mesh=mesh,
        in_specs=(field, field, field, cell, cell, cell),
        out_specs=(field, field),
        check_vma=False,
    )
```

```python
import functools
import jax
import jax.numpy as jnp
from jax import lax
from jax.experimental import pallas as pl
from jax.experimental.pallas import tpu as pltpu
from jax.sharding import PartitionSpec as P

STEPS = 5
NPML = 8
DT = 0.5
DAMPING = 0.1
STRENGTH = 3.0
SMAX = 0.8
DENOM = 1.0 + DAMPING * DT / 2.0
KEEP = (1.0 - DAMPING * DT / 2.0) / DENOM

LANES = 128
ROWS = 8
SIDE = 8
SLOT = 2 * SIDE
GUARD = 8
VMEM_LIMIT = 8 * 1024 * 1024

EX, HX, PX, EPS, RES = 0, 3, 6, 9, 10
ARRAYS = 11

COST = 3_000_000


def faces(count):
    up, down = [], []
    last = count - STEPS
    for c in range(3):
        up.append((EX + c, last, STEPS))
        down.append((EX + c, 0, STEPS if c > 0 else STEPS - 1))
    for c in range(3):
        up.append((HX + c, last if c > 0 else last + 1, STEPS if c > 0 else STEPS - 1))
        down.append((HX + c, 0, STEPS - 1))
    for c in range(3):
        up.append((PX + c, last + 1, STEPS - 1))
        down.append((PX + c, 0, STEPS - 1 if c > 0 else STEPS - 2))
    for a in (EPS, RES):
        up.append((a, last + 1, STEPS - 1))
        down.append((a, 0, STEPS - 1))
    return up, down


def planes_of(parts):
    return sum(count for _, _, count in parts)


def pick(refs, array):
    e_ref, h_ref, p_ref, eps_ref, res_ref = refs
    if array < HX:
        return e_ref.at[array]
    if array < PX:
        return h_ref.at[array - HX]
    if array < EPS:
        return p_ref.at[array - PX]
    return eps_ref if array == EPS else res_ref


def pack_faces(e_ref, h_ref, p_ref, eps_ref, freq_ref, mark_ref, up_ref, down_ref, side_ref, res_ref):
    xcount, zcount, ycount = eps_ref.shape
    core = lax.axis_index("gz")
    shape = (zcount, zcount)
    diagonal = lax.broadcasted_iota(jnp.int32, shape, 0) == lax.broadcasted_iota(jnp.int32, shape, 1)
    for x in range(xcount):
        for j in range(ycount // LANES):
            lanes = slice(j * LANES, (j + 1) * LANES)
            row = jnp.broadcast_to(mark_ref[x, j : j + 1, :].astype(jnp.float32), shape)
            mark = jnp.sum(jnp.where(diagonal, row, 0.0), axis=1, keepdims=True)
            freq = freq_ref[x, :, lanes] * DT
            res_ref[x, :, lanes] = mark * (freq * freq / DENOM)
    refs = (e_ref, h_ref, p_ref, eps_ref, res_ref)
    for parts, out_ref in zip(faces(xcount), (up_ref, down_ref)):
        at = 0
        for array, first, count in parts:
            out_ref[at : at + count] = pick(refs, array)[first : first + count]
            at += count
    begin = pl.multiple_of((1 - core) * (zcount - ROWS), ROWS)
    for array in range(ARRAYS):
        side_ref[array] = pick(refs, array)[:, pl.ds(begin, ROWS), :]


def slots():
    lane = lax.broadcasted_iota(jnp.int32, (ROWS, LANES), 1)
    return lane, lane // SLOT, lane % SLOT < SIDE


def turn(value, shift):
    shift = shift % LANES
    return pltpu.roll(value, shift, 1) if shift else value


def pack_strips(e_ref, h_ref, p_ref, eps_ref, res_ref, side_ref, low_ref, high_ref):
    xcount, zcount, ycount = eps_ref.shape
    core = lax.axis_index("gz")
    refs = (e_ref, h_ref, p_ref, eps_ref, res_ref)
    own = pl.multiple_of(core * ROWS, ROWS)
    halo = pl.multiple_of((1 - core) * zcount, ROWS)
    lane, slot, left = slots()
    per = LANES // SLOT
    assert per < xcount <= 2 * per and xcount - STEPS >= per >= STEPS
    for array in range(ARRAYS):
        src = pick(refs, array)
        for z in range(0, zcount + ROWS, ROWS):
            packed = [jnp.zeros((ROWS, LANES), jnp.float32)] * 2
            for x in range(xcount):
                if z < zcount:
                    first, last = src[x, z : z + ROWS, 0:LANES], src[x, z : z + ROWS, ycount - LANES : ycount]
                else:
                    first, last = side_ref[array, x, :, 0:LANES], side_ref[array, x, :, ycount - LANES : ycount]
                ends = turn(jnp.where(lane < SIDE, first, last), SLOT * (x % per) + SIDE)
                packed[x // per] = jnp.where(slot == x % per, ends, packed[x // per])
            rows = pl.ds(own + z, ROWS) if z < zcount else pl.ds(halo, ROWS)
            low_ref[array, rows, :] = jnp.where(left, turn(packed[1], -SIDE), packed[0])
            high_ref[array, rows, :] = jnp.where(left, packed[0], turn(packed[1], SIDE))


def merge_strips(ahead_ref, behind_ref, low_ref, high_ref):
    _, _, left = slots()
    for array in range(ARRAYS):
        for t in range(ahead_ref.shape[1] // ROWS):
            rows = slice(t * ROWS, (t + 1) * ROWS)
            ahead, behind = ahead_ref[array, rows, :], behind_ref[array, rows, :]
            low_ref[array, rows, :] = jnp.where(left, behind, ahead)
            high_ref[array, rows, :] = jnp.where(left, turn(behind, -SIDE), turn(ahead, SIDE))


def profile(index, total):
    depth = jnp.maximum(NPML - index, 0.0) + jnp.maximum(index - (total - 1 - NPML), 0.0)
    return SMAX * (depth / NPML) ** 3


class Block:
    def __init__(self, shape, state):
        self.xcount, self.zcount, self.ycount = shape
        self.E, self.H, self.R, self.U, self.EC, self.EB, self.BM, self.HC, self.HB = state
        self.tiles = self.ycount // LANES
        self.extent = self.xcount + 2 * STEPS
        self.zsteps = self.zcount // ROWS + 1
        core = lax.axis_index("gz")
        self.own = pl.multiple_of(GUARD + core * ROWS, ROWS)
        self.halo = pl.multiple_of(GUARD + (1 - core) * self.zcount, ROWS)
        self.near = pl.multiple_of(core * (self.zcount - ROWS), ROWS)
        self.lane = lax.broadcasted_iota(jnp.int32, (ROWS, LANES), 1)

    def put(self, array, plane, row, j, value):
        rows = pl.ds(row, ROWS)
        if array < HX:
            self.E[array, plane, j, rows, :] = value
        elif array < PX:
            self.H[array - HX, plane, j, rows, :] = value * (1.0 / 6.0)
        elif array < EPS:
            self.R[array - PX, plane, j, rows, :] = value * (1.0 / 3.0)
        elif array == EPS:
            self.EC[plane, j, rows, :] = value
        else:
            self.BM[plane, j, rows, :] = value

    def put_ends(self, array, plane, packed, slot):
        for t in range(self.zsteps):
            ends = turn(packed[array, t * ROWS : (t + 1) * ROWS, :], -(SLOT * slot + SIDE))
            self.put(array, plane, GUARD + t * ROWS, self.tiles, ends)

    def place(self, x, j):
        xtotal = self.xcount * lax.axis_size("gx")
        ytotal = self.ycount * lax.axis_size("gy")
        yplace = lax.axis_index("gy") * self.ycount
        xpos = lax.axis_index("gx") * self.xcount + x - STEPS
        lane = self.lane
        inside = jnp.full((ROWS, LANES), (xpos >= 0) & (xpos < xtotal))
        if j < self.tiles:
            ypos = yplace + j * LANES + lane
        else:
            ypos = yplace + jnp.where(lane < SIDE, self.ycount + lane, lane - LANES)
            inside = inside & ((lane < SIDE) | (lane >= LANES - SIDE)) & (ypos >= 0) & (ypos < ytotal)
        xsigma = profile(jnp.full((ROWS, LANES), xpos, jnp.int32).astype(jnp.float32), xtotal)
        return (xsigma + profile(ypos.astype(jnp.float32), ytotal)) * (DT / 2.0), inside

    def magnetic_coefficients(self, x):
        for j in range(self.tiles + 1):
            half, inside = self.place(x, j)
            over = 1.0 / (1.0 + half)
            self.HC[x, j] = jnp.where(inside, (1.0 - half) * over, 0.0)
            self.HB[x, j] = jnp.where(inside, (DT / 6.0) * over, 0.0)

    def electric_coefficients(self, x):
        for j in range(self.tiles + 1):
            half, inside = self.place(x, j)
            for t in range(self.zsteps):
                rows = pl.ds(GUARD + t * ROWS, ROWS)
                eps = self.EC[x, j, rows, :]
                over = 1.0 / jnp.where(inside, eps + half, 1.0)
                self.EC[x, j, rows, :] = jnp.where(inside, (eps - half) * over, 0.0)
                self.EB[x, j, rows, :] = jnp.where(inside, (6.0 * DT) * over, 0.0)

    def guards(self, x):
        zero = jnp.zeros((ROWS, LANES), jnp.float32)
        end = GUARD + self.zsteps * ROWS
        for j in range(self.tiles + 1):
            for c in range(3):
                self.H[c, x, j, 0:GUARD, :] = zero
                self.E[c, x, j, end : end + ROWS, :] = zero

    def load(self, ref, c, x, row):
        return [ref[c, x, j, pl.ds(row, ROWS), :] for j in range(self.tiles + 1)]

    def next_lane(self, v):
        r = [turn(t, -1) for t in v]
        return [jnp.where(self.lane == LANES - 1, r[(j + 1) % len(v)], r[j]) for j in range(len(v))]

    def previous_lane(self, v):
        r = [turn(t, 1) for t in v]
        return [jnp.where(self.lane == 0, r[j - 1], r[j]) for j in range(len(v))]

    def magnetic(self, x):
        E, H = self.E, self.H
        for t in range(self.zsteps):
            row = GUARD + t * ROWS
            rows = pl.ds(row, ROWS)
            ex, ey, ez = (self.load(E, c, x, row) for c in range(3))
            ex_z, ey_z = (self.load(E, c, x, row + 1) for c in (0, 1))
            ey_x, ez_x = (self.load(E, c, x + 1, row) for c in (1, 2))
            ex_y, ez_y = self.next_lane(ex), self.next_lane(ez)
            for j in range(self.tiles + 1):
                hc, hb = self.HC[x, j], self.HB[x, j]
                curls = (
                    (ez_y[j] - ez[j]) - (ey_z[j] - ey[j]),
                    (ex_z[j] - ex[j]) - (ez_x[j] - ez[j]),
                    (ey_x[j] - ey[j]) - (ex_y[j] - ex[j]),
                )
                for c in range(3):
                    H[c, x, j, rows, :] = hc * H[c, x, j, rows, :] - hb * curls[c]

    def electric(self, x, step):
        E, H, R, U = self.E, self.H, self.R, self.U
        last = step == STEPS
        for t in range(self.zsteps - 1 if last else self.zsteps):
            row = self.own + t * ROWS if last else GUARD + t * ROWS
            rows = pl.ds(row, ROWS)
            hx, hy, hz = (self.load(H, c, x, row) for c in range(3))
            hx_z, hy_z = (self.load(H, c, x, row - 1) for c in (0, 1))
            hy_x, hz_x = (self.load(H, c, x - 1, row) for c in (1, 2))
            hx_y, hz_y = self.previous_lane(hx), self.previous_lane(hz)
            for j in range(self.tiles if last else self.tiles + 1):
                ec, eb, bm = (ref[x, j, rows, :] for ref in (self.EC, self.EB, self.BM))
                curls = (
                    (hz[j] - hz_y[j]) - (hy[j] - hy_z[j]),
                    (hx[j] - hx_z[j]) - (hz[j] - hz_x[j]),
                    (hy[j] - hy_x[j]) - (hx[j] - hx_y[j]),
                )
                for c in range(3):
                    e, r = E[c, x, j, rows, :], R[c, x, j, rows, :]
                    u = bm * (e - r)
                    if step > 1:
                        u = KEEP * U[c, x, j, rows, :] + u
                    if not last:
                        U[c, x, j, rows, :] = u
                        R[c, x, j, rows, :] = r + u
                    E[c, x, j, rows, :] = ec * e + eb * (curls[c] - u)


def loop(begin, end, act, unroll):
    def run(x, carry):
        act(x)
        return carry

    lax.fori_loop(begin, end, run, 0, unroll=unroll)


def prepare(e_ref, h_ref, p_ref, eps_ref, res_ref, side_ref, low_ref, high_ref, *state):
    block = Block(eps_ref.shape, state)
    refs = (e_ref, h_ref, p_ref, eps_ref, res_ref)
    per = LANES // SLOT
    for array in range(ARRAYS):
        src = pick(refs, array)

        def own_plane(x, array=array, src=src):
            for j in range(block.tiles):
                lanes = slice(j * LANES, (j + 1) * LANES)
                for z in range(0, block.zcount, ROWS):
                    block.put(array, x + STEPS, block.own + z, j, src[x, z : z + ROWS, lanes])
                block.put(array, x + STEPS, block.halo, j, side_ref[array, x, :, lanes])

        loop(0, block.xcount, own_plane, 4)
        for x in range(block.xcount):
            block.put_ends(array, x + STEPS, low_ref if x < per else high_ref, x % per)
    loop(0, block.extent, block.guards, 1)
    loop(0, block.extent, block.magnetic_coefficients, 2)
    loop(STEPS, STEPS + block.xcount, block.electric_coefficients, 2)


def inner(shape, *state):
    block = Block(shape, state[len(state) // 2 :])
    for step in range(1, STEPS + 1):
        loop(STEPS + step - 1, STEPS + block.xcount - step, block.magnetic, 4)
        loop(STEPS + step, STEPS + block.xcount - step, functools.partial(block.electric, step=step), 4)


def outer(shape, low_ref, low_side_ref, high_ref, high_side_ref, corner_low_ref, corner_high_ref, *rest):
    count = (len(rest) - 2) // 2
    e_out, h_out = rest[count : count + 2]
    block = Block(shape, rest[count + 2 :])
    xcount, zcount = block.xcount, block.zcount
    per = LANES // SLOT
    ups, downs = faces(xcount)
    for parts, face, face_side, corner, above in (
        (ups, low_ref, low_side_ref, corner_low_ref, False),
        (downs, high_ref, high_side_ref, corner_high_ref, True),
    ):
        at = 0
        for array, first, count in parts:
            for i in range(count):
                plane = xcount + STEPS + i if above else first + i - (xcount - STEPS)
                for j in range(block.tiles):
                    lanes = slice(j * LANES, (j + 1) * LANES)
                    for z in range(0, zcount, ROWS):
                        block.put(array, plane, block.own + z, j, face[at + i, z : z + ROWS, lanes])
                    block.put(array, plane, block.halo, j, face_side[at + i, pl.ds(block.near, ROWS), lanes])
                block.put_ends(array, plane, corner, first + i if above else first + i - per)
            at += count
    zero = jnp.zeros((ROWS, LANES), jnp.float32)
    for j in range(block.tiles + 1):
        for t in range(block.zsteps):
            rows = pl.ds(GUARD + t * ROWS, ROWS)
            block.H[0, 0, j, rows, :] = zero
            block.E[0, block.extent - 1, j, rows, :] = zero
            block.R[0, block.extent - 2, j, rows, :] = zero
    loop(1, STEPS, block.electric_coefficients, STEPS - 1)
    loop(STEPS + xcount, block.extent - 1, block.electric_coefficients, STEPS - 1)
    for step in range(1, STEPS + 1):
        above = xcount + STEPS - step

        def both(x, act, gap):
            act(x)
            act(x + gap)

        low = step - 1
        loop(low, low + STEPS, functools.partial(both, act=block.magnetic, gap=above - low), STEPS)
        act = functools.partial(block.electric, step=step)
        loop(step, step + STEPS, functools.partial(both, act=act, gap=above - step), STEPS)

    def finish(x):
        for c in range(3):
            for j in range(block.tiles):
                lanes = slice(j * LANES, (j + 1) * LANES)
                for z in range(0, zcount, ROWS):
                    rows = pl.ds(block.own + z, ROWS)
                    e_out[c, x, z : z + ROWS, lanes] = block.E[c, x + STEPS, j, rows, :]
                    h_out[c, x, z : z + ROWS, lanes] = block.H[c, x + STEPS, j, rows, :] * 6.0

    loop(0, xcount, finish, 2)


def call(kernel, outs, args, flops, aliases=None):
    vmem = pl.BlockSpec(memory_space=pltpu.VMEM)
    return pl.pallas_call(
        kernel,
        out_shape=outs,
        in_specs=[vmem] * len(args),
        out_specs=[vmem] * len(outs),
        input_output_aliases=aliases or {},
        cost_estimate=pl.CostEstimate(flops=flops, bytes_accessed=flops, transcendentals=0),
        compiler_params=pltpu.CompilerParams(vmem_limit_bytes=VMEM_LIMIT),
    )(*[pltpu.with_memory_space_constraint(a, pltpu.VMEM) for a in args])


def shift(value, axis, by):
    count = lax.axis_size(axis)
    return lax.ppermute(value, axis, [(i, i + by) for i in range(count) if 0 <= i + by < count])


def swap(value):
    return lax.ppermute(value, "gz", [(0, 1), (1, 0)])


def kept(*shape):
    return pltpu.VMEM(shape, jnp.float32)


def body(e_field, h_field, polar, permittivity, resonance, dispersive):
    xcount, zcount, ycount = shape = permittivity.shape
    ups, downs = faces(xcount)
    up, down, side, res = call(
        pack_faces,
        [
            kept(planes_of(ups), zcount, ycount),
            kept(planes_of(downs), zcount, ycount),
            kept(ARRAYS, xcount, ROWS, ycount),
            kept(xcount, zcount, ycount),
        ],
        (e_field, h_field, polar, permittivity, resonance, jnp.swapaxes(dispersive, 1, 2)),
        COST,
    )
    side = swap(side)
    low, high = shift(up, "gx", 1), shift(down, "gx", -1)
    fields = (e_field, h_field, polar, permittivity, res, side)
    strips = [kept(ARRAYS, zcount + ROWS, LANES)] * 2
    first, last = call(pack_strips, strips, fields, COST)
    ahead, behind = shift(first, "gy", -1), shift(last, "gy", 1)
    strip_low, strip_high = call(merge_strips, strips, (ahead, behind), COST)
    corner_low, corner_high = shift(strip_high, "gx", 1), shift(strip_low, "gx", -1)
    extent, tiles, rows = xcount + 2 * STEPS, ycount // LANES + 1, zcount + ROWS + 2 * GUARD
    state = [kept(3, extent, tiles, rows, LANES)] * 4
    state += [kept(extent, tiles, rows, LANES)] * 3 + [kept(extent, tiles, ROWS, LANES)] * 2
    count = len(state)
    kept_state = call(prepare, state, (*fields, strip_low, strip_high), 3 * COST)
    low, high, kept_state = lax.optimization_barrier((low, high, kept_state))
    low_side, high_side = swap(low), swap(high)
    kept_state = call(functools.partial(inner, shape), state, kept_state, 6 * COST, {i: i for i in range(count)})
    faces_in = (low, low_side, high, high_side, corner_low, corner_high)
    given = len(faces_in)
    outs = [jax.ShapeDtypeStruct(e_field.shape, jnp.float32), jax.ShapeDtypeStruct(h_field.shape, jnp.float32)]
    aliases = {given + i: 2 + i for i in range(count)}
    return tuple(call(functools.partial(outer, shape), outs + state, (*faces_in, *kept_state), 6 * COST, aliases)[:2])


def solution(mesh):
    field, cell = P(None, "gx", "gz", "gy"), P("gx", "gz", "gy")
    return jax.shard_map(
        body,
        mesh=mesh,
        in_specs=(field, field, field, cell, cell, cell),
        out_specs=(field, field),
        check_vma=False,
    )
```

```python
import functools
import jax
import jax.numpy as jnp
from jax import lax
from jax.experimental import pallas as pl
from jax.experimental.pallas import tpu as pltpu
from jax.sharding import PartitionSpec as P

STEPS = 5
SPLIT = 4
NPML = 8
DT = 0.5
DAMPING = 0.1
STRENGTH = 3.0
SMAX = 0.8
DENOM = 1.0 + DAMPING * DT / 2.0
KEEP = (1.0 - DAMPING * DT / 2.0) / DENOM

LANES = 128
ROWS = 8
SIDE = 8
SLOT = 2 * SIDE
GUARD = 8
VMEM_LIMIT = 8 * 1024 * 1024

EX, HX, PX, EPS, RES = 0, 3, 6, 9, 10
ARRAYS = 11

COST = 3_000_000


def faces():
    parts = [(EX + c, STEPS) for c in range(3)]
    parts += [(HX + c, STEPS if c > 0 else STEPS - 1) for c in range(3)]
    parts += [(a, STEPS - 1) for a in (PX, PX + 1, PX + 2, EPS, RES)]
    return parts


def planes_of(parts):
    return sum(count for _, count in parts)


def pick(refs, array):
    e_ref, h_ref, p_ref, eps_ref, res_ref = refs
    if array < HX:
        return e_ref.at[array]
    if array < PX:
        return h_ref.at[array - HX]
    if array < EPS:
        return p_ref.at[array - PX]
    return eps_ref if array == EPS else res_ref


def even(axis):
    return lax.axis_index(axis) % 2 == 0


def pack_faces(
    e_hbm, h_hbm, p_hbm, eps_hbm, freq_hbm, mark_hbm,
    first_ref, second_ref, side_ref, e_ref, h_ref, p_ref, eps_ref, res_ref,
    freq_ref, mark_ref, arrived,
):
    xcount, zcount, ycount = eps_ref.shape
    moves = [
        pltpu.make_async_copy(src, dst, arrived.at[i])
        for i, (src, dst) in enumerate(
            (
                (mark_hbm, mark_ref),
                (freq_hbm, freq_ref),
                (eps_hbm, eps_ref),
                (e_hbm, e_ref),
                (h_hbm, h_ref),
                (p_hbm, p_ref),
            )
        )
    ]
    for move in moves:
        move.start()
    core = lax.axis_index("gz")
    shape = (zcount, zcount)
    diagonal = lax.broadcasted_iota(jnp.int32, shape, 0) == lax.broadcasted_iota(jnp.int32, shape, 1)
    moves[0].wait()
    moves[1].wait()
    for x in range(xcount):
        for j in range(ycount // LANES):
            lanes = slice(j * LANES, (j + 1) * LANES)
            row = jnp.broadcast_to(mark_ref[x, j : j + 1, :].astype(jnp.float32), shape)
            mark = jnp.sum(jnp.where(diagonal, row, 0.0), axis=1, keepdims=True)
            freq = freq_ref[x, :, lanes] * DT
            res_ref[x, :, lanes] = mark * (freq * freq / DENOM)
    for move in moves[2:]:
        move.wait()
    refs = (e_ref, h_ref, p_ref, eps_ref, res_ref)
    for up, out_ref in ((even("gx"), first_ref), (jnp.logical_not(even("gx")), second_ref)):
        at = 0
        for array, count in faces():
            for i in range(count):
                out_ref[at + i] = pick(refs, array)[jnp.where(up, xcount - 1 - i, i)]
            at += count
    begin = pl.multiple_of((1 - core) * (zcount - ROWS), ROWS)
    for array in range(ARRAYS):
        side_ref[array] = pick(refs, array)[:, pl.ds(begin, ROWS), :]


def slots():
    lane = lax.broadcasted_iota(jnp.int32, (ROWS, LANES), 1)
    return lane, lane // SLOT, lane % SLOT < SIDE


def turn(value, shift):
    shift = shift % LANES
    return pltpu.roll(value, shift, 1) if shift else value


def pack_strips(e_ref, h_ref, p_ref, eps_ref, res_ref, side_ref, first_ref, second_ref):
    xcount, zcount, ycount = eps_ref.shape
    core = lax.axis_index("gz")
    refs = (e_ref, h_ref, p_ref, eps_ref, res_ref)
    own = pl.multiple_of(core * ROWS, ROWS)
    halo = pl.multiple_of((1 - core) * zcount, ROWS)
    lane, slot, left = slots()
    per = LANES // SLOT
    assert xcount == 2 * per and per >= STEPS
    up = even("gy")
    for array in range(ARRAYS):
        src = pick(refs, array)
        for z in range(0, zcount + ROWS, ROWS):
            packed = [jnp.zeros((ROWS, LANES), jnp.float32)] * 2
            for x in range(xcount):
                if z < zcount:
                    first, last = src[x, z : z + ROWS, 0:LANES], src[x, z : z + ROWS, ycount - LANES : ycount]
                else:
                    first, last = side_ref[array, x, :, 0:LANES], side_ref[array, x, :, ycount - LANES : ycount]
                ends = turn(jnp.where(lane < SIDE, first, last), SLOT * (x % per) + SIDE)
                packed[x // per] = jnp.where(slot == x % per, ends, packed[x // per])
            rows = pl.ds(own + z, ROWS) if z < zcount else pl.ds(halo, ROWS)
            low = jnp.where(left, turn(packed[1], -SIDE), packed[0])
            high = jnp.where(left, packed[0], turn(packed[1], SIDE))
            first_ref[array, rows, :] = jnp.where(up, high, low)
            second_ref[array, rows, :] = jnp.where(up, low, high)


def merge_strips(first_ref, second_ref, low_ref, high_ref, corner_first_ref, corner_second_ref):
    _, _, left = slots()
    up, over = even("gy"), even("gx")
    for array in range(ARRAYS):
        for t in range(first_ref.shape[1] // ROWS):
            rows = slice(t * ROWS, (t + 1) * ROWS)
            first, second = first_ref[array, rows, :], second_ref[array, rows, :]
            ahead, behind = jnp.where(up, first, second), jnp.where(up, second, first)
            low = jnp.where(left, behind, ahead)
            high = jnp.where(left, turn(behind, -SIDE), turn(ahead, SIDE))
            low_ref[array, rows, :] = low
            high_ref[array, rows, :] = high
            corner_first_ref[array, rows, :] = jnp.where(over, high, low)
            corner_second_ref[array, rows, :] = jnp.where(over, low, high)


def profile(index, total):
    depth = jnp.maximum(NPML - index, 0.0) + jnp.maximum(index - (total - 1 - NPML), 0.0)
    return SMAX * (depth / NPML) ** 3


class Block:
    def __init__(self, shape, state):
        self.xcount, self.zcount, self.ycount = shape
        self.E, self.H, self.R, self.U, self.EC, self.EB, self.BM, self.HC, self.HB = state
        self.tiles = self.ycount // LANES
        self.extent = self.xcount + 2 * STEPS
        self.zsteps = self.zcount // ROWS + 1
        core = lax.axis_index("gz")
        self.own = pl.multiple_of(GUARD + core * ROWS, ROWS)
        self.halo = pl.multiple_of(GUARD + (1 - core) * self.zcount, ROWS)
        self.near = pl.multiple_of(core * (self.zcount - ROWS), ROWS)
        self.lane = lax.broadcasted_iota(jnp.int32, (ROWS, LANES), 1)

    def put(self, array, plane, row, j, value):
        rows = pl.ds(row, ROWS)
        if array < HX:
            self.E[array, plane, j, rows, :] = value
        elif array < PX:
            self.H[array - HX, plane, j, rows, :] = value * (1.0 / 6.0)
        elif array < EPS:
            self.R[array - PX, plane, j, rows, :] = value * (1.0 / 3.0)
        elif array == EPS:
            self.EC[plane, j, rows, :] = value
        else:
            self.BM[plane, j, rows, :] = value

    def put_ends(self, array, plane, packed, slot):
        for t in range(self.zsteps):
            ends = pltpu.roll(packed[array, t * ROWS : (t + 1) * ROWS, :], LANES - SIDE - SLOT * slot, 1)
            self.put(array, plane, GUARD + t * ROWS, self.tiles, ends)

    def place(self, x, j):
        xtotal = self.xcount * lax.axis_size("gx")
        ytotal = self.ycount * lax.axis_size("gy")
        yplace = lax.axis_index("gy") * self.ycount
        xpos = lax.axis_index("gx") * self.xcount + x - STEPS
        lane = self.lane
        inside = jnp.full((ROWS, LANES), (xpos >= 0) & (xpos < xtotal))
        if j < self.tiles:
            ypos = yplace + j * LANES + lane
        else:
            ypos = yplace + jnp.where(lane < SIDE, self.ycount + lane, lane - LANES)
            inside = inside & ((lane < SIDE) | (lane >= LANES - SIDE)) & (ypos >= 0) & (ypos < ytotal)
        xsigma = profile(jnp.full((ROWS, LANES), xpos, jnp.int32).astype(jnp.float32), xtotal)
        return (xsigma + profile(ypos.astype(jnp.float32), ytotal)) * (DT / 2.0), inside

    def magnetic_coefficients(self, x):
        for j in range(self.tiles + 1):
            half, inside = self.place(x, j)
            over = 1.0 / (1.0 + half)
            self.HC[x, j] = jnp.where(inside, (1.0 - half) * over, 0.0)
            self.HB[x, j] = jnp.where(inside, (DT / 6.0) * over, 0.0)

    def electric_coefficients(self, x):
        for j in range(self.tiles + 1):
            half, inside = self.place(x, j)
            for t in range(self.zsteps):
                rows = pl.ds(GUARD + t * ROWS, ROWS)
                eps = self.EC[x, j, rows, :]
                over = 1.0 / jnp.where(inside, eps + half, 1.0)
                self.EC[x, j, rows, :] = jnp.where(inside, (eps - half) * over, 0.0)
                self.EB[x, j, rows, :] = jnp.where(inside, (6.0 * DT) * over, 0.0)

    def guards(self, x):
        zero = jnp.zeros((ROWS, LANES), jnp.float32)
        end = GUARD + self.zsteps * ROWS
        for j in range(self.tiles + 1):
            for c in range(3):
                self.H[c, x, j, 0:GUARD, :] = zero
                self.E[c, x, j, end : end + ROWS, :] = zero

    def load(self, ref, c, x, row):
        return [ref[c, x, j, pl.ds(row, ROWS), :] for j in range(self.tiles + 1)]

    def next_lane(self, v):
        r = [turn(t, -1) for t in v]
        return [jnp.where(self.lane == LANES - 1, r[(j + 1) % len(v)], r[j]) for j in range(len(v))]

    def previous_lane(self, v):
        r = [turn(t, 1) for t in v]
        return [jnp.where(self.lane == 0, r[j - 1], r[j]) for j in range(len(v))]

    def magnetic(self, x):
        E, H = self.E, self.H
        for t in range(self.zsteps):
            row = GUARD + t * ROWS
            rows = pl.ds(row, ROWS)
            ex, ey, ez = (self.load(E, c, x, row) for c in range(3))
            ex_z, ey_z = (self.load(E, c, x, row + 1) for c in (0, 1))
            ey_x, ez_x = (self.load(E, c, x + 1, row) for c in (1, 2))
            ex_y, ez_y = self.next_lane(ex), self.next_lane(ez)
            for j in range(self.tiles + 1):
                hc, hb = self.HC[x, j], self.HB[x, j]
                curls = (
                    (ez_y[j] - ez[j]) - (ey_z[j] - ey[j]),
                    (ex_z[j] - ex[j]) - (ez_x[j] - ez[j]),
                    (ey_x[j] - ey[j]) - (ex_y[j] - ex[j]),
                )
                for c in range(3):
                    H[c, x, j, rows, :] = hc * H[c, x, j, rows, :] - hb * curls[c]

    def electric(self, x, step):
        E, H, R, U = self.E, self.H, self.R, self.U
        last = step == STEPS
        for t in range(self.zsteps - 1 if last else self.zsteps):
            row = self.own + t * ROWS if last else GUARD + t * ROWS
            rows = pl.ds(row, ROWS)
            hx, hy, hz = (self.load(H, c, x, row) for c in range(3))
            hx_z, hy_z = (self.load(H, c, x, row - 1) for c in (0, 1))
            hy_x, hz_x = (self.load(H, c, x - 1, row) for c in (1, 2))
            hx_y, hz_y = self.previous_lane(hx), self.previous_lane(hz)
            for j in range(self.tiles if last else self.tiles + 1):
                ec, eb, bm = (ref[x, j, rows, :] for ref in (self.EC, self.EB, self.BM))
                curls = (
                    (hz[j] - hz_y[j]) - (hy[j] - hy_z[j]),
                    (hx[j] - hx_z[j]) - (hz[j] - hz_x[j]),
                    (hy[j] - hy_x[j]) - (hx[j] - hx_y[j]),
                )
                for c in range(3):
                    e, r = E[c, x, j, rows, :], R[c, x, j, rows, :]
                    u = bm * (e - r)
                    if step > 1:
                        u = KEEP * U[c, x, j, rows, :] + u
                    if not last:
                        U[c, x, j, rows, :] = u
                        R[c, x, j, rows, :] = r + u
                    E[c, x, j, rows, :] = ec * e + eb * (curls[c] - u)


def loop(begin, end, act, unroll):
    def run(x, carry):
        act(x)
        return carry

    lax.fori_loop(begin, end, run, 0, unroll=unroll)


def prepare(e_ref, h_ref, p_ref, eps_ref, res_ref, side_ref, *state):
    block = Block(eps_ref.shape, state)
    refs = (e_ref, h_ref, p_ref, eps_ref, res_ref)
    for array in range(ARRAYS):
        src = pick(refs, array)

        def own_plane(x, array=array, src=src):
            for j in range(block.tiles):
                lanes = slice(j * LANES, (j + 1) * LANES)
                for z in range(0, block.zcount, ROWS):
                    block.put(array, x + STEPS, block.own + z, j, src[x, z : z + ROWS, lanes])
                block.put(array, x + STEPS, block.halo, j, side_ref[array, x, :, lanes])

        loop(0, block.xcount, own_plane, 4)
    loop(0, block.extent, block.guards, 1)
    loop(0, block.extent, block.magnetic_coefficients, 2)


def prepare_ends(shape, low_ref, high_ref, *states):
    block = Block(shape, states[len(states) // 2 :])
    per = LANES // SLOT
    for array in range(ARRAYS):
        for x in range(block.xcount):
            block.put_ends(array, x + STEPS, low_ref if x < per else high_ref, x % per)
    loop(STEPS, STEPS + block.xcount, block.electric_coefficients, 2)


def inner(shape, begin, end, *states):
    block = Block(shape, states[len(states) // 2 :])
    for step in range(begin, end):
        loop(STEPS + step - 1, STEPS + block.xcount - step, block.magnetic, 4)
        loop(STEPS + step, STEPS + block.xcount - step, functools.partial(block.electric, step=step), 4)


def outer(
    shape, first_ref, first_side_ref, second_ref, second_side_ref, corner_first_ref, corner_second_ref, *rest
):
    count = (len(rest) - 2) // 2
    e_out, h_out = rest[count : count + 2]
    block = Block(shape, rest[count + 2 :])
    xcount, zcount = block.xcount, block.zcount
    per = LANES // SLOT
    for above, face, face_side, corner in (
        (even("gx"), first_ref, first_side_ref, corner_first_ref),
        (jnp.logical_not(even("gx")), second_ref, second_side_ref, corner_second_ref),
    ):
        at = 0
        for array, count in faces():
            for i in range(count):
                plane = jnp.where(above, xcount + STEPS + i, STEPS - 1 - i)
                for j in range(block.tiles):
                    lanes = slice(j * LANES, (j + 1) * LANES)
                    for z in range(0, zcount, ROWS):
                        block.put(array, plane, block.own + z, j, face[at + i, z : z + ROWS, lanes])
                    block.put(array, plane, block.halo, j, face_side[at + i, pl.ds(block.near, ROWS), lanes])
                block.put_ends(array, plane, corner, jnp.where(above, i, per - 1 - i))
            at += count
    loop(1, STEPS, block.electric_coefficients, STEPS - 1)
    loop(STEPS + xcount, block.extent - 1, block.electric_coefficients, STEPS - 1)
    for step in range(1, STEPS + 1):
        above = xcount + STEPS - step

        def both(x, act, gap):
            act(x)
            act(x + gap)

        low = step - 1
        loop(low, low + STEPS, functools.partial(both, act=block.magnetic, gap=above - low), STEPS)
        act = functools.partial(block.electric, step=step)
        loop(step, step + STEPS, functools.partial(both, act=act, gap=above - step), STEPS)

    def finish(x):
        for c in range(3):
            for j in range(block.tiles):
                lanes = slice(j * LANES, (j + 1) * LANES)
                for z in range(0, zcount, ROWS):
                    rows = pl.ds(block.own + z, ROWS)
                    e_out[c, x, z : z + ROWS, lanes] = block.E[c, x + STEPS, j, rows, :]
                    h_out[c, x, z : z + ROWS, lanes] = block.H[c, x + STEPS, j, rows, :] * 6.0

    loop(0, xcount, finish, 2)


def call(kernel, outs, args, cost, aliases=None, scratch=(), spec=pltpu.VMEM):
    args = [pltpu.with_memory_space_constraint(a, spec) for a in args]
    work = int(cost * COST)
    return pl.pallas_call(
        kernel,
        out_shape=outs,
        in_specs=[pl.BlockSpec(memory_space=spec)] * len(args),
        out_specs=[pl.BlockSpec(memory_space=pltpu.VMEM)] * len(outs),
        scratch_shapes=scratch,
        input_output_aliases=aliases or {},
        cost_estimate=pl.CostEstimate(flops=work, bytes_accessed=work, transcendentals=0),
        compiler_params=pltpu.CompilerParams(vmem_limit_bytes=VMEM_LIMIT),
    )(*args)


def swap(value, axis, begin=0):
    pairs = [(i, i + 1) for i in range(begin, lax.axis_size(axis) - 1, 2)]
    return lax.ppermute(value, axis, pairs + [(b, a) for a, b in pairs])


def kept(*shape):
    return pltpu.VMEM(shape, jnp.float32)


def body(e_field, h_field, polar, permittivity, resonance, dispersive):
    xcount, zcount, ycount = shape = permittivity.shape
    marks = jnp.swapaxes(dispersive, 1, 2)
    face = kept(planes_of(faces()), zcount, ycount)
    first, second, side, *fields = call(
        pack_faces,
        [face, face, kept(ARRAYS, xcount, ROWS, ycount)]
        + [kept(*a.shape) for a in (e_field, h_field, polar, permittivity, resonance)],
        (e_field, h_field, polar, permittivity, resonance, marks),
        1,
        scratch=[
            pltpu.VMEM(shape, jnp.float32),
            pltpu.VMEM(marks.shape, marks.dtype),
            pltpu.SemaphoreType.DMA((6,)),
        ],
        spec=pltpu.HBM,
    )
    side = swap(side, "gz")
    second, first = swap(second, "gx", 1), swap(first, "gx")
    fields = (*fields, side)
    strip = kept(ARRAYS, zcount + ROWS, LANES)
    strips = call(pack_strips, [strip] * 2, fields, 1)
    *strips, fields = lax.optimization_barrier((*strips, fields))
    strip_second, strip_first = swap(strips[1], "gy", 1), swap(strips[0], "gy")
    extent, tiles, rows = xcount + 2 * STEPS, ycount // LANES + 1, zcount + ROWS + 2 * GUARD
    states = [kept(3, extent, tiles, rows, LANES)] * 4
    states += [kept(extent, tiles, rows, LANES)] * 3 + [kept(extent, tiles, ROWS, LANES)] * 2
    count = len(states)
    state = call(prepare, states, fields, 2)
    low, high, corner_first, corner_second = call(merge_strips, [strip] * 4, (strip_first, strip_second), 0.2)
    corner_second, corner_first = swap(corner_second, "gx", 1), swap(corner_first, "gx")
    ends = functools.partial(prepare_ends, shape)
    state = call(ends, states, (low, high, *state), 0.1, {2 + i: i for i in range(count)})
    same = {i: i for i in range(count)}
    state = call(functools.partial(inner, shape, 1, SPLIT), states, state, 0.1, same)
    barrier = (first, second, corner_first, corner_second, state)
    first, second, corner_first, corner_second, state = lax.optimization_barrier(barrier)
    first_side, second_side = swap(first, "gz"), swap(second, "gz")
    state = call(functools.partial(inner, shape, SPLIT, STEPS + 1), states, state, 0.1, same)
    arrived = (first, first_side, second, second_side, corner_first, corner_second)
    given = len(arrived)
    outs = [jax.ShapeDtypeStruct(e_field.shape, jnp.float32), jax.ShapeDtypeStruct(h_field.shape, jnp.float32)]
    aliases = {given + i: 2 + i for i in range(count)}
    return tuple(call(functools.partial(outer, shape), outs + states, (*arrived, *state), 1, aliases)[:2])


def solution(mesh):
    field, cell = P(None, "gx", "gz", "gy"), P("gx", "gz", "gy")
    return jax.shard_map(
        body,
        mesh=mesh,
        in_specs=(field, field, field, cell, cell, cell),
        out_specs=(field, field),
        check_vma=False,
    )
```

```python
import functools
import jax
import jax.numpy as jnp
from jax import lax
from jax.experimental import pallas as pl
from jax.experimental.pallas import tpu as pltpu
from jax.sharding import PartitionSpec as P

STEPS = 5
SPLIT = 3
AHEAD = 2
GROUP = 8
NPML = 8
DT = 0.5
DAMPING = 0.1
STRENGTH = 3.0
SMAX = 0.8
DENOM = 1.0 + DAMPING * DT / 2.0
KEEP = (1.0 - DAMPING * DT / 2.0) / DENOM

LANES = 128
ROWS = 8
SIDE = 8
SLOT = 2 * SIDE
GUARD = 8
VMEM_LIMIT = 8 * 1024 * 1024

EX, HX, PX, EPS, RES = 0, 3, 6, 9, 10
ARRAYS = 11

COST = 3_000_000


def faces():
    parts = [(EX + c, STEPS) for c in range(3)]
    parts += [(HX + c, STEPS if c > 0 else STEPS - 1) for c in range(3)]
    parts += [(a, STEPS - 1) for a in (PX, PX + 1, PX + 2, EPS, RES)]
    return parts


def planes_of(parts):
    return sum(count for _, count in parts)


def pick(refs, array):
    e_ref, h_ref, p_ref, eps_ref, res_ref = refs
    if array < HX:
        return e_ref.at[array]
    if array < PX:
        return h_ref.at[array - HX]
    if array < EPS:
        return p_ref.at[array - PX]
    return eps_ref if array == EPS else res_ref


def even(axis):
    return lax.axis_index(axis) % 2 == 0


def pack_faces(
    e_hbm, h_hbm, p_hbm, eps_hbm, freq_hbm, mark_hbm,
    first_ref, second_ref, side_ref, e_ref, h_ref, p_ref, eps_ref, res_ref,
    freq_ref, mark_ref, arrived,
):
    xcount, zcount, ycount = eps_ref.shape
    xcount = eps_ref.shape[0]
    pairs = ((mark_hbm, mark_ref), (freq_hbm, freq_ref), (eps_hbm, eps_ref))
    pairs += ((e_hbm, e_ref), (h_hbm, h_ref), (p_hbm, p_ref))
    moves = [pltpu.make_async_copy(src, dst, arrived.at[i]) for i, (src, dst) in enumerate(pairs)]
    for move in moves:
        move.start()
    refs = (e_ref, h_ref, p_ref, eps_ref, res_ref)
    begin = pl.multiple_of((1 - lax.axis_index("gz")) * (zcount - ROWS), ROWS)

    def pack(arrays):
        for up, out_ref in ((even("gx"), first_ref), (jnp.logical_not(even("gx")), second_ref)):
            at = 0
            for array, count in faces():
                for i in range(count if array in arrays else 0):
                    out_ref[at + i] = pick(refs, array)[jnp.where(up, xcount - 1 - i, i)]
                at += count
        for array in arrays:
            side_ref[array] = pick(refs, array)[:, pl.ds(begin, ROWS), :]

    shape = (zcount, zcount)
    diagonal = lax.broadcasted_iota(jnp.int32, shape, 0) == lax.broadcasted_iota(jnp.int32, shape, 1)
    moves[0].wait()
    moves[1].wait()
    for x in range(xcount):
        for j in range(ycount // LANES):
            lanes = slice(j * LANES, (j + 1) * LANES)
            row = jnp.broadcast_to(mark_ref[x, j : j + 1, :].astype(jnp.float32), shape)
            mark = jnp.sum(jnp.where(diagonal, row, 0.0), axis=1, keepdims=True)
            freq = freq_ref[x, :, lanes] * DT
            res_ref[x, :, lanes] = mark * (freq * freq / DENOM)
    moves[2].wait()
    pack((EPS, RES))
    for move, array in zip(moves[3:], (EX, HX, PX)):
        move.wait()
        pack(range(array, array + 3))


def slots():
    lane = lax.broadcasted_iota(jnp.int32, (ROWS, LANES), 1)
    return lane, lane // SLOT, lane % SLOT < SIDE


def turn(value, shift):
    shift = shift % LANES
    return pltpu.roll(value, shift, 1) if shift else value


def pack_strips(e_ref, h_ref, p_ref, eps_ref, res_ref, side_ref, first_ref, second_ref):
    xcount, zcount, ycount = eps_ref.shape
    core = lax.axis_index("gz")
    refs = (e_ref, h_ref, p_ref, eps_ref, res_ref)
    own = pl.multiple_of(core * ROWS, ROWS)
    halo = pl.multiple_of((1 - core) * zcount, ROWS)
    lane, slot, left = slots()
    per = LANES // SLOT
    assert xcount == 2 * per and per >= STEPS
    up = even("gy")
    zs = range(0, zcount + ROWS, ROWS)
    for array in range(ARRAYS):
        src = pick(refs, array)
        packed = [[None, None] for _ in zs]
        for x in range(xcount):
            for n, z in enumerate(zs):
                if z < zcount:
                    first, last = src[x, z : z + ROWS, 0:LANES], src[x, z : z + ROWS, ycount - LANES : ycount]
                else:
                    first, last = side_ref[array, x, :, 0:LANES], side_ref[array, x, :, ycount - LANES : ycount]
                ends = turn(jnp.where(lane < SIDE, first, last), SLOT * (x % per) + SIDE)
                before = packed[n][x // per]
                packed[n][x // per] = ends if before is None else jnp.where(slot == x % per, ends, before)
        for n, z in enumerate(zs):
            p = packed[n]
            rows = pl.ds(own + z, ROWS) if z < zcount else pl.ds(halo, ROWS)
            low = jnp.where(left, turn(p[1], -SIDE), p[0])
            high = jnp.where(left, p[0], turn(p[1], SIDE))
            first_ref[array, rows, :] = jnp.where(up, high, low)
            second_ref[array, rows, :] = jnp.where(up, low, high)


def merge_strips(first_ref, second_ref, low_ref, high_ref, corner_first_ref, corner_second_ref):
    _, _, left = slots()
    up, over = even("gy"), even("gx")
    for array in range(ARRAYS):
        for t in range(first_ref.shape[1] // ROWS):
            rows = slice(t * ROWS, (t + 1) * ROWS)
            first, second = first_ref[array, rows, :], second_ref[array, rows, :]
            ahead, behind = jnp.where(up, first, second), jnp.where(up, second, first)
            low = jnp.where(left, behind, ahead)
            high = jnp.where(left, turn(behind, -SIDE), turn(ahead, SIDE))
            low_ref[array, rows, :] = low
            high_ref[array, rows, :] = high
            corner_first_ref[array, rows, :] = jnp.where(over, high, low)
            corner_second_ref[array, rows, :] = jnp.where(over, low, high)


def profile(index, total):
    depth = jnp.maximum(NPML - index, 0.0) + jnp.maximum(index - (total - 1 - NPML), 0.0)
    return SMAX * (depth / NPML) ** 3


class Block:
    def __init__(self, shape, state):
        self.xcount, self.zcount, self.ycount = shape
        self.E, self.H, self.R, self.U, self.EC, self.EB, self.BM, self.HC, self.HB = state
        self.tiles = self.ycount // LANES
        self.extent = self.xcount + 2 * STEPS
        self.zsteps = self.zcount // ROWS + 1
        core = lax.axis_index("gz")
        self.own = pl.multiple_of(GUARD + core * ROWS, ROWS)
        self.halo = pl.multiple_of(GUARD + (1 - core) * self.zcount, ROWS)
        self.near = pl.multiple_of(core * (self.zcount - ROWS), ROWS)
        self.lane = lax.broadcasted_iota(jnp.int32, (ROWS, LANES), 1)

    def put(self, array, plane, row, j, value):
        rows = pl.ds(row, ROWS)
        if array < HX:
            self.E[array, plane, j, rows, :] = value
        elif array < PX:
            self.H[array - HX, plane, j, rows, :] = value * (1.0 / 6.0)
        elif array < EPS:
            self.R[array - PX, plane, j, rows, :] = value * (1.0 / 3.0)
        elif array == EPS:
            self.EC[plane, j, rows, :] = value
        else:
            self.BM[plane, j, rows, :] = value

    def put_ends(self, array, plane, packed, slot):
        for t in range(self.zsteps):
            ends = pltpu.roll(packed[array, t * ROWS : (t + 1) * ROWS, :], LANES - SIDE - SLOT * slot, 1)
            self.put(array, plane, GUARD + t * ROWS, self.tiles, ends)

    def place(self, x, j):
        xtotal = self.xcount * lax.axis_size("gx")
        ytotal = self.ycount * lax.axis_size("gy")
        yplace = lax.axis_index("gy") * self.ycount
        xpos = lax.axis_index("gx") * self.xcount + x - STEPS
        lane = self.lane
        inside = jnp.full((ROWS, LANES), (xpos >= 0) & (xpos < xtotal))
        if j < self.tiles:
            ypos = yplace + j * LANES + lane
        else:
            ypos = yplace + jnp.where(lane < SIDE, self.ycount + lane, lane - LANES)
            inside = inside & ((lane < SIDE) | (lane >= LANES - SIDE)) & (ypos >= 0) & (ypos < ytotal)
        xsigma = profile(jnp.full((ROWS, LANES), xpos, jnp.int32).astype(jnp.float32), xtotal)
        return (xsigma + profile(ypos.astype(jnp.float32), ytotal)) * (DT / 2.0), inside

    def magnetic_coefficients(self, x):
        for j in range(self.tiles + 1):
            half, inside = self.place(x, j)
            over = 1.0 / (1.0 + half)
            self.HC[x, j] = jnp.where(inside, (1.0 - half) * over, 0.0)
            self.HB[x, j] = jnp.where(inside, (DT / 6.0) * over, 0.0)

    def electric_coefficients(self, x, columns):
        for j in columns:
            half, inside = self.place(x, j)
            for t in range(self.zsteps):
                rows = pl.ds(GUARD + t * ROWS, ROWS)
                eps = self.EC[x, j, rows, :]
                over = 1.0 / jnp.where(inside, eps + half, 1.0)
                self.EC[x, j, rows, :] = jnp.where(inside, (eps - half) * over, 0.0)
                self.EB[x, j, rows, :] = jnp.where(inside, (6.0 * DT) * over, 0.0)

    def guards(self, x):
        zero = jnp.zeros((ROWS, LANES), jnp.float32)
        end = GUARD + self.zsteps * ROWS
        for j in range(self.tiles + 1):
            for c in range(3):
                self.H[c, x, j, 0:GUARD, :] = zero
                self.E[c, x, j, end : end + ROWS, :] = zero

    def load(self, ref, c, x, row):
        return [ref[c, x, j, pl.ds(row, ROWS), :] for j in range(self.tiles + 1)]

    def next_lane(self, v):
        r = [turn(t, -1) for t in v]
        return [jnp.where(self.lane == LANES - 1, r[(j + 1) % len(v)], r[j]) for j in range(len(v))]

    def previous_lane(self, v):
        r = [turn(t, 1) for t in v]
        return [jnp.where(self.lane == 0, r[j - 1], r[j]) for j in range(len(v))]

    def magnetic(self, *planes):
        E, H = self.E, self.H
        places = [(x, GUARD + t * ROWS) for x in planes for t in range(self.zsteps)]
        rolled = {}

        def turned(n):
            x, row = places[n]
            rolled[n] = [self.next_lane(self.load(E, c, x, row)) for c in (0, 2)]

        for n in range(min(AHEAD, len(places))):
            turned(n)
        for n, (x, row) in enumerate(places):
            if n + AHEAD < len(places):
                turned(n + AHEAD)
            rows = pl.ds(row, ROWS)
            ex, ey, ez = (self.load(E, c, x, row) for c in range(3))
            ex_z, ey_z = (self.load(E, c, x, row + 1) for c in (0, 1))
            ey_x, ez_x = (self.load(E, c, x + 1, row) for c in (1, 2))
            ex_y, ez_y = rolled.pop(n)
            for j in range(self.tiles + 1):
                hc, hb = self.HC[x, j], self.HB[x, j]
                curls = (
                    (ez_y[j] - ez[j]) - (ey_z[j] - ey[j]),
                    (ex_z[j] - ex[j]) - (ez_x[j] - ez[j]),
                    (ey_x[j] - ey[j]) - (ex_y[j] - ex[j]),
                )
                for c in range(3):
                    H[c, x, j, rows, :] = hc * H[c, x, j, rows, :] - hb * curls[c]

    def electric(self, *planes, step, out=None):
        E, H, R, U = self.E, self.H, self.R, self.U
        last = step == STEPS
        zsteps = range(self.zsteps - 1 if last else self.zsteps)
        places = [(x, self.own + t * ROWS if last else GUARD + t * ROWS) for x in planes for t in zsteps]
        rolled = {}

        def turned(n):
            x, row = places[n]
            rolled[n] = [self.previous_lane(self.load(H, c, x, row)) for c in (0, 2)]

        for n in range(min(AHEAD, len(places))):
            turned(n)
        for n, (x, row) in enumerate(places):
            if n + AHEAD < len(places):
                turned(n + AHEAD)
            rows = pl.ds(row, ROWS)
            hx, hy, hz = (self.load(H, c, x, row) for c in range(3))
            hx_z, hy_z = (self.load(H, c, x, row - 1) for c in (0, 1))
            hy_x, hz_x = (self.load(H, c, x - 1, row) for c in (1, 2))
            hx_y, hz_y = rolled.pop(n)
            for j in range(self.tiles if last else self.tiles + 1):
                ec, eb, bm = (ref[x, j, rows, :] for ref in (self.EC, self.EB, self.BM))
                curls = (
                    (hz[j] - hz_y[j]) - (hy[j] - hy_z[j]),
                    (hx[j] - hx_z[j]) - (hz[j] - hz_x[j]),
                    (hy[j] - hy_x[j]) - (hx[j] - hx_y[j]),
                )
                for c in range(3):
                    e, r = E[c, x, j, rows, :], R[c, x, j, rows, :]
                    u = bm * (e - r)
                    if step > 1:
                        u = KEEP * U[c, x, j, rows, :] + u
                    if not last:
                        U[c, x, j, rows, :] = u
                        R[c, x, j, rows, :] = r + u
                    value = ec * e + eb * (curls[c] - u)
                    if out is None:
                        E[c, x, j, rows, :] = value
                    else:
                        z = (n % len(zsteps)) * ROWS
                        out[c, x - STEPS, z : z + ROWS, j * LANES : (j + 1) * LANES] = value


def groups(begin, end, act, size):
    whole = (end - begin) // size

    def run(n, carry):
        x = begin + n * size
        act(*(x + i for i in range(size)))
        return carry

    if whole > 1:
        lax.fori_loop(0, whole, run, 0)
    elif whole:
        act(*range(begin, begin + size))
    if begin + whole * size < end:
        act(*range(begin + whole * size, end))


def loop(begin, end, act, unroll):
    def run(x, carry):
        act(x)
        return carry

    lax.fori_loop(begin, end, run, 0, unroll=unroll)


def prepare(e_ref, h_ref, p_ref, eps_ref, res_ref, side_ref, *state):
    block = Block(eps_ref.shape, state)
    refs = (e_ref, h_ref, p_ref, eps_ref, res_ref)
    for array in range(ARRAYS):
        src = pick(refs, array)

        def own_plane(x, array=array, src=src):
            for j in range(block.tiles):
                lanes = slice(j * LANES, (j + 1) * LANES)
                for z in range(0, block.zcount, ROWS):
                    block.put(array, x + STEPS, block.own + z, j, src[x, z : z + ROWS, lanes])
                block.put(array, x + STEPS, block.halo, j, side_ref[array, x, :, lanes])

        loop(0, block.xcount, own_plane, 4)
    loop(0, block.extent, block.guards, 1)
    loop(0, block.extent, block.magnetic_coefficients, 2)
    coefficients = functools.partial(block.electric_coefficients, columns=range(block.tiles))
    loop(STEPS, STEPS + block.xcount, coefficients, 2)


def prepare_ends(shape, low_ref, high_ref, *states):
    block = Block(shape, states[len(states) // 2 :])
    per = LANES // SLOT
    for array in range(ARRAYS):
        for x in range(block.xcount):
            block.put_ends(array, x + STEPS, low_ref if x < per else high_ref, x % per)
    coefficients = functools.partial(block.electric_coefficients, columns=(block.tiles,))
    loop(STEPS, STEPS + block.xcount, coefficients, 2)


def groups(begin, end, act, size):
    whole = (end - begin) // size

    def run(n, carry):
        x = begin + n * size
        act(*(x + i for i in range(size)))
        return carry

    if whole > 1:
        lax.fori_loop(0, whole, run, 0)
    elif whole:
        act(*range(begin, begin + size))
    if begin + whole * size < end:
        act(*range(begin + whole * size, end))


def inner(shape, begin, end, *states):
    block = Block(shape, states[len(states) // 2 :])
    for step in range(begin, end):
        last = STEPS + block.xcount - step
        groups(STEPS + step - 1, last, block.magnetic, GROUP)
        groups(STEPS + step, last, functools.partial(block.electric, step=step), GROUP)


def arrivals(block, first, second):
    per = LANES // SLOT
    for above, refs in ((even("gx"), first), (jnp.logical_not(even("gx")), second)):
        at = 0
        for array, count in faces():
            for i in range(count):
                plane = jnp.where(above, block.xcount + STEPS + i, STEPS - 1 - i)
                yield array, plane, at + i, jnp.where(above, i, per - 1 - i), *refs
            at += count


def inner_end(shape, first_ref, second_ref, corner_first_ref, corner_second_ref, *states):
    inner(shape, SPLIT, STEPS + 1, *states)
    block = Block(shape, states[len(states) // 2 :])
    came = arrivals(block, (first_ref, corner_first_ref), (second_ref, corner_second_ref))
    for array, plane, at, slot, face, corner in came:
        for j in range(block.tiles):
            for z in range(0, block.zcount, ROWS):
                block.put(array, plane, block.own + z, j, face[at, z : z + ROWS, j * LANES : (j + 1) * LANES])
        block.put_ends(array, plane, corner, slot)


def outer(shape, first_side_ref, second_side_ref, *rest):
    e_stage, h_stage, sent = rest[-3:]
    count = (len(rest) - 5) // 2
    e_out, h_out = rest[count : count + 2]
    block = Block(shape, rest[count + 2 : -3])
    xcount, zcount = block.xcount, block.zcount
    moves = []

    def send(stage, out, begin, end):
        part = slice(begin - STEPS, end - STEPS)
        move = pltpu.make_async_copy(stage.at[:, part], out.at[:, part], sent.at[len(moves)])
        move.start()
        moves.append(move)

    def stage(ref, into, scale, begin, end):
        for x in range(begin, end):
            for c in range(3):
                for j in range(block.tiles):
                    lanes = slice(j * LANES, (j + 1) * LANES)
                    for z in range(0, zcount, ROWS):
                        value = ref[c, x, j, pl.ds(block.own + z, ROWS), :]
                        into[c, x - STEPS, z : z + ROWS, lanes] = value if scale is None else value * scale

    middle = (2 * STEPS, xcount)
    stage(block.E, e_stage, None, *middle)
    send(e_stage, e_out, *middle)
    stage(block.H, h_stage, 6.0, *middle)
    send(h_stage, h_out, *middle)
    for array, plane, at, _, side in arrivals(block, (first_side_ref,), (second_side_ref,)):
        for j in range(block.tiles):
            value = side[at, pl.ds(block.near, ROWS), j * LANES : (j + 1) * LANES]
            block.put(array, plane, block.halo, j, value)
    coefficients = functools.partial(block.electric_coefficients, columns=range(block.tiles + 1))
    loop(1, STEPS, coefficients, STEPS - 1)
    loop(STEPS + xcount, block.extent - 1, coefficients, STEPS - 1)
    for step in range(1, STEPS + 1):
        above = xcount + STEPS - step
        block.magnetic(*range(step - 1, step - 1 + STEPS), *range(above, above + STEPS))
        act = functools.partial(block.electric, step=step)
        low, high = range(step, step + STEPS), range(above, above + STEPS)
        if step < STEPS:
            act(*low, *high)
        else:
            for part in (low, high):
                stage(block.H, h_stage, 6.0, part.start, part.stop)
                send(h_stage, h_out, part.start, part.stop)
                act(*part, out=e_stage)
                send(e_stage, e_out, part.start, part.stop)
    for move in moves:
        move.wait()


def call(kernel, outs, args, cost, aliases=None, scratch=(), spec=pltpu.VMEM, hbm=0):
    args = [pltpu.with_memory_space_constraint(a, spec) for a in args]
    work = int(cost * COST)
    return pl.pallas_call(
        kernel,
        out_shape=outs,
        in_specs=[pl.BlockSpec(memory_space=spec)] * len(args),
        out_specs=[pl.BlockSpec(memory_space=pltpu.HBM if i < hbm else pltpu.VMEM) for i in range(len(outs))],
        scratch_shapes=scratch,
        input_output_aliases=aliases or {},
        cost_estimate=pl.CostEstimate(flops=work, bytes_accessed=work, transcendentals=0),
        compiler_params=pltpu.CompilerParams(vmem_limit_bytes=VMEM_LIMIT),
    )(*args)


def swap(value, axis, begin=0):
    pairs = [(i, i + 1) for i in range(begin, lax.axis_size(axis) - 1, 2)]
    return lax.ppermute(value, axis, pairs + [(b, a) for a, b in pairs])


def kept(*shape):
    return pltpu.VMEM(shape, jnp.float32)


def body(e_field, h_field, polar, permittivity, resonance, dispersive):
    xcount, zcount, ycount = shape = permittivity.shape
    marks = jnp.swapaxes(dispersive, 1, 2)
    face = kept(planes_of(faces()), zcount, ycount)
    first, second, side, *fields = call(
        pack_faces,
        [face, face, kept(ARRAYS, xcount, ROWS, ycount)]
        + [kept(*a.shape) for a in (e_field, h_field, polar, permittivity, resonance)],
        (e_field, h_field, polar, permittivity, resonance, marks),
        1,
        scratch=[
            pltpu.VMEM(shape, jnp.float32),
            pltpu.VMEM(marks.shape, marks.dtype),
            pltpu.SemaphoreType.DMA((6,)),
        ],
        spec=pltpu.HBM,
    )
    side = swap(side, "gz")
    second, first = swap(second, "gx", 1), swap(first, "gx")
    fields = (*fields, side)
    strip = kept(ARRAYS, zcount + ROWS, LANES)
    strips = call(pack_strips, [strip] * 2, fields, 1)
    *strips, fields = lax.optimization_barrier((*strips, fields))
    strip_second, strip_first = swap(strips[1], "gy", 1), swap(strips[0], "gy")
    extent, tiles, rows = xcount + 2 * STEPS, ycount // LANES + 1, zcount + ROWS + 2 * GUARD
    states = [kept(3, extent, tiles, rows, LANES)] * 4
    states += [kept(extent, tiles, rows, LANES)] * 3 + [kept(extent, tiles, ROWS, LANES)] * 2
    count = len(states)
    state = call(prepare, states, fields, 2)
    strip_first, strip_second, state = lax.optimization_barrier((strip_first, strip_second, state))
    low, high, corner_first, corner_second = call(merge_strips, [strip] * 4, (strip_first, strip_second), 0.2)
    corner_second, corner_first = swap(corner_second, "gx", 1), swap(corner_first, "gx")
    ends = functools.partial(prepare_ends, shape)
    state = call(ends, states, (low, high, *state), 0.1, {2 + i: i for i in range(count)})
    same = {i: i for i in range(count)}
    state = call(functools.partial(inner, shape, 1, SPLIT), states, state, 0.1, same)
    barrier = (first, second, corner_first, corner_second, state)
    first, second, corner_first, corner_second, state = lax.optimization_barrier(barrier)
    first_side, second_side = swap(first, "gz"), swap(second, "gz")
    came = (first, second, corner_first, corner_second)
    given = len(came)
    aliases = {given + i: i for i in range(count)}
    state = call(functools.partial(inner_end, shape), states, (*came, *state), 0.1, aliases)
    outs = [jax.ShapeDtypeStruct(e_field.shape, jnp.float32), jax.ShapeDtypeStruct(h_field.shape, jnp.float32)]
    scratch = [pltpu.VMEM(e_field.shape, jnp.float32)] * 2 + [pltpu.SemaphoreType.DMA((6,))]
    aliases = {2 + i: 2 + i for i in range(count)}
    ends = (first_side, second_side, *state)
    return tuple(call(functools.partial(outer, shape), outs + states, ends, 1, aliases, scratch, hbm=2)[:2])


def solution(mesh):
    field, cell = P(None, "gx", "gz", "gy"), P("gx", "gz", "gy")
    return jax.shard_map(
        body,
        mesh=mesh,
        in_specs=(field, field, field, cell, cell, cell),
        out_specs=(field, field),
        check_vma=False,
    )
```

```python
import functools
import jax
import jax.numpy as jnp
from jax import lax
from jax.experimental import pallas as pl
from jax.experimental.pallas import tpu as pltpu
from jax.sharding import PartitionSpec as P

STEPS = 5
AHEAD = 2
GROUP = 8
NPML = 8
DT = 0.5
DAMPING = 0.1
STRENGTH = 3.0
SMAX = 0.8
DENOM = 1.0 + DAMPING * DT / 2.0
KEEP = (1.0 - DAMPING * DT / 2.0) / DENOM

LANES = 128
ROWS = 8
SIDE = 8
SLOT = 2 * SIDE
GUARD = 8
VMEM_LIMIT = 8 * 1024 * 1024

EX, HX, PX, EPS, RES = 0, 3, 6, 9, 10
ARRAYS = 11

COST = 3_000_000


def faces():
    parts = [(EX + c, STEPS) for c in range(3)]
    parts += [(HX + c, STEPS if c > 0 else STEPS - 1) for c in range(3)]
    parts += [(a, STEPS - 1) for a in (PX, PX + 1, PX + 2, EPS, RES)]
    return parts


def planes_of(parts):
    return sum(count for _, count in parts)


def pick(refs, array):
    e_ref, h_ref, p_ref, eps_ref, res_ref = refs
    if array < HX:
        return e_ref.at[array]
    if array < PX:
        return h_ref.at[array - HX]
    if array < EPS:
        return p_ref.at[array - PX]
    return eps_ref if array == EPS else res_ref


def even(axis):
    return lax.axis_index(axis) % 2 == 0


def pack_faces(
    e_hbm, h_hbm, p_hbm, eps_hbm, freq_hbm, mark_hbm,
    first_ref, second_ref, side_ref, e_ref, h_ref, p_ref, eps_ref, res_ref,
    freq_ref, mark_ref, arrived,
):
    xcount, zcount, ycount = eps_ref.shape
    xcount = eps_ref.shape[0]
    pairs = ((mark_hbm, mark_ref), (freq_hbm, freq_ref), (eps_hbm, eps_ref))
    pairs += ((e_hbm, e_ref), (h_hbm, h_ref), (p_hbm, p_ref))
    moves = [pltpu.make_async_copy(src, dst, arrived.at[i]) for i, (src, dst) in enumerate(pairs)]
    for move in moves:
        move.start()
    refs = (e_ref, h_ref, p_ref, eps_ref, res_ref)
    begin = pl.multiple_of((1 - lax.axis_index("gz")) * (zcount - ROWS), ROWS)

    def pack(arrays):
        for up, out_ref in ((even("gx"), first_ref), (jnp.logical_not(even("gx")), second_ref)):
            at = 0
            for array, count in faces():
                for i in range(count if array in arrays else 0):
                    out_ref[at + i] = pick(refs, array)[jnp.where(up, xcount - 1 - i, i)]
                at += count
        for array in arrays:
            side_ref[array] = pick(refs, array)[:, pl.ds(begin, ROWS), :]

    shape = (zcount, zcount)
    diagonal = lax.broadcasted_iota(jnp.int32, shape, 0) == lax.broadcasted_iota(jnp.int32, shape, 1)
    moves[0].wait()
    moves[1].wait()
    for x in range(xcount):
        for j in range(ycount // LANES):
            lanes = slice(j * LANES, (j + 1) * LANES)
            row = jnp.broadcast_to(mark_ref[x, j : j + 1, :].astype(jnp.float32), shape)
            mark = jnp.sum(jnp.where(diagonal, row, 0.0), axis=1, keepdims=True)
            freq = freq_ref[x, :, lanes] * DT
            res_ref[x, :, lanes] = mark * (freq * freq / DENOM)
    moves[2].wait()
    pack((EPS, RES))
    for move, array in zip(moves[3:], (EX, HX, PX)):
        move.wait()
        pack(range(array, array + 3))


def slots():
    lane = lax.broadcasted_iota(jnp.int32, (ROWS, LANES), 1)
    return lane, lane // SLOT, lane % SLOT < SIDE


def turn(value, shift):
    shift = shift % LANES
    return pltpu.roll(value, shift, 1) if shift else value


def pack_strips(e_ref, h_ref, p_ref, eps_ref, res_ref, side_ref, first_ref, second_ref):
    xcount, zcount, ycount = eps_ref.shape
    core = lax.axis_index("gz")
    refs = (e_ref, h_ref, p_ref, eps_ref, res_ref)
    own = pl.multiple_of(core * ROWS, ROWS)
    halo = pl.multiple_of((1 - core) * zcount, ROWS)
    lane, slot, left = slots()
    per = LANES // SLOT
    assert xcount == 2 * per and per >= STEPS
    up = even("gy")
    zs = range(0, zcount + ROWS, ROWS)
    for array in range(ARRAYS):
        src = pick(refs, array)
        packed = [[None, None] for _ in zs]
        for x in range(xcount):
            for n, z in enumerate(zs):
                if z < zcount:
                    first, last = src[x, z : z + ROWS, 0:LANES], src[x, z : z + ROWS, ycount - LANES : ycount]
                else:
                    first, last = side_ref[array, x, :, 0:LANES], side_ref[array, x, :, ycount - LANES : ycount]
                ends = turn(jnp.where(lane < SIDE, first, last), SLOT * (x % per) + SIDE)
                before = packed[n][x // per]
                packed[n][x // per] = ends if before is None else jnp.where(slot == x % per, ends, before)
        for n, z in enumerate(zs):
            p = packed[n]
            rows = pl.ds(own + z, ROWS) if z < zcount else pl.ds(halo, ROWS)
            low = jnp.where(left, turn(p[1], -SIDE), p[0])
            high = jnp.where(left, p[0], turn(p[1], SIDE))
            first_ref[array, rows, :] = jnp.where(up, high, low)
            second_ref[array, rows, :] = jnp.where(up, low, high)


def merge_strips(first_ref, second_ref, low_ref, high_ref, corner_first_ref, corner_second_ref):
    _, slot, left = slots()
    up, over = even("gy"), even("gx")
    per = LANES // SLOT
    for t in range(first_ref.shape[1] // ROWS):
        rows = slice(t * ROWS, (t + 1) * ROWS)
        packed = ([None] * (corner_rows() + 1), [None] * (corner_rows() + 1))
        for array in range(ARRAYS):
            first, second = first_ref[array, rows, :], second_ref[array, rows, :]
            ahead, behind = jnp.where(up, first, second), jnp.where(up, second, first)
            low = jnp.where(left, behind, ahead)
            high = jnp.where(left, turn(behind, -SIDE), turn(ahead, SIDE))
            low_ref[array, rows, :] = low
            high_ref[array, rows, :] = high
            at, place = divmod(STEPS * array, per)
            begin, end = turn(low, SLOT * place), turn(high, SLOT * (place - per + STEPS))
            for into, value in zip(packed, (jnp.where(over, end, begin), jnp.where(over, begin, end))):
                into[at] = value if into[at] is None else jnp.where(slot >= place, value, into[at])
                into[at + 1] = value if place + STEPS > per else None
        for into, out_ref in zip(packed, (corner_first_ref, corner_second_ref)):
            for n in range(corner_rows()):
                out_ref[n, rows, :] = into[n]


def corner_rows():
    return -(-STEPS * ARRAYS // (LANES // SLOT))


def profile(index, total):
    depth = jnp.maximum(NPML - index, 0.0) + jnp.maximum(index - (total - 1 - NPML), 0.0)
    return SMAX * (depth / NPML) ** 3


class Block:
    def __init__(self, shape, state):
        self.xcount, self.zcount, self.ycount = shape
        self.E, self.H, self.R, self.U, self.EC, self.EB, self.BM, self.HC, self.HB = state
        self.tiles = self.ycount // LANES
        self.extent = self.xcount + 2 * STEPS
        self.zsteps = self.zcount // ROWS + 1
        core = lax.axis_index("gz")
        self.own = pl.multiple_of(GUARD + core * ROWS, ROWS)
        self.halo = pl.multiple_of(GUARD + (1 - core) * self.zcount, ROWS)
        self.lane = lax.broadcasted_iota(jnp.int32, (ROWS, LANES), 1)

    def put(self, array, plane, row, j, value):
        rows = pl.ds(row, ROWS)
        if array < HX:
            self.E[array, plane, j, rows, :] = value
        elif array < PX:
            self.H[array - HX, plane, j, rows, :] = value * (1.0 / 6.0)
        elif array < EPS:
            self.R[array - PX, plane, j, rows, :] = value * (1.0 / 3.0)
        elif array == EPS:
            self.EC[plane, j, rows, :] = value
        else:
            self.BM[plane, j, rows, :] = value

    def put_ends(self, array, plane, packed, slot, row=None):
        for t in range(self.zsteps):
            ends = pltpu.roll(packed[array if row is None else row, t * ROWS : (t + 1) * ROWS, :], LANES - SIDE - SLOT * slot, 1)
            self.put(array, plane, GUARD + t * ROWS, self.tiles, ends)

    def place(self, x, j):
        xtotal = self.xcount * lax.axis_size("gx")
        ytotal = self.ycount * lax.axis_size("gy")
        yplace = lax.axis_index("gy") * self.ycount
        xpos = lax.axis_index("gx") * self.xcount + x - STEPS
        lane = self.lane
        inside = jnp.full((ROWS, LANES), (xpos >= 0) & (xpos < xtotal))
        if j < self.tiles:
            ypos = yplace + j * LANES + lane
        else:
            ypos = yplace + jnp.where(lane < SIDE, self.ycount + lane, lane - LANES)
            inside = inside & ((lane < SIDE) | (lane >= LANES - SIDE)) & (ypos >= 0) & (ypos < ytotal)
        xsigma = profile(jnp.full((ROWS, LANES), xpos, jnp.int32).astype(jnp.float32), xtotal)
        return (xsigma + profile(ypos.astype(jnp.float32), ytotal)) * (DT / 2.0), inside

    def magnetic_coefficients(self, x):
        for j in range(self.tiles + 1):
            half, inside = self.place(x, j)
            over = 1.0 / (1.0 + half)
            self.HC[x, j] = jnp.where(inside, (1.0 - half) * over, 0.0)
            self.HB[x, j] = jnp.where(inside, (DT / 6.0) * over, 0.0)

    def electric_coefficients(self, x, columns, at=None):
        for j in columns:
            half, inside = self.place(x, j)
            for row in at or range(GUARD, GUARD + self.zsteps * ROWS, ROWS):
                rows = pl.ds(row, ROWS)
                eps = self.EC[x, j, rows, :]
                over = 1.0 / jnp.where(inside, eps + half, 1.0)
                self.EC[x, j, rows, :] = jnp.where(inside, (eps - half) * over, 0.0)
                self.EB[x, j, rows, :] = jnp.where(inside, (6.0 * DT) * over, 0.0)

    def guards(self, x):
        zero = jnp.zeros((ROWS, LANES), jnp.float32)
        end = GUARD + self.zsteps * ROWS
        for j in range(self.tiles + 1):
            for c in range(3):
                self.H[c, x, j, 0:GUARD, :] = zero
                self.E[c, x, j, end : end + ROWS, :] = zero

    def load(self, ref, c, x, row):
        return [ref[c, x, j, pl.ds(row, ROWS), :] for j in range(self.tiles + 1)]

    def next_lane(self, v):
        r = [turn(t, -1) for t in v]
        return [jnp.where(self.lane == LANES - 1, r[(j + 1) % len(v)], r[j]) for j in range(len(v))]

    def previous_lane(self, v):
        r = [turn(t, 1) for t in v]
        return [jnp.where(self.lane == 0, r[j - 1], r[j]) for j in range(len(v))]

    def magnetic(self, *planes):
        E, H = self.E, self.H
        places = [(x, GUARD + t * ROWS) for x in planes for t in range(self.zsteps)]
        rolled = {}

        def turned(n):
            x, row = places[n]
            rolled[n] = [self.next_lane(self.load(E, c, x, row)) for c in (0, 2)]

        for n in range(min(AHEAD, len(places))):
            turned(n)
        for n, (x, row) in enumerate(places):
            if n + AHEAD < len(places):
                turned(n + AHEAD)
            rows = pl.ds(row, ROWS)
            ex, ey, ez = (self.load(E, c, x, row) for c in range(3))
            ex_z, ey_z = (self.load(E, c, x, row + 1) for c in (0, 1))
            ey_x, ez_x = (self.load(E, c, x + 1, row) for c in (1, 2))
            ex_y, ez_y = rolled.pop(n)
            for j in range(self.tiles + 1):
                hc, hb = self.HC[x, j], self.HB[x, j]
                curls = (
                    (ez_y[j] - ez[j]) - (ey_z[j] - ey[j]),
                    (ex_z[j] - ex[j]) - (ez_x[j] - ez[j]),
                    (ey_x[j] - ey[j]) - (ex_y[j] - ex[j]),
                )
                for c in range(3):
                    H[c, x, j, rows, :] = hc * H[c, x, j, rows, :] - hb * curls[c]

    def electric(self, *planes, step, out=None):
        E, H, R, U = self.E, self.H, self.R, self.U
        last = step == STEPS
        zsteps = range(self.zsteps - 1 if last else self.zsteps)
        places = [(x, self.own + t * ROWS if last else GUARD + t * ROWS) for x in planes for t in zsteps]
        rolled = {}

        def turned(n):
            x, row = places[n]
            rolled[n] = [self.previous_lane(self.load(H, c, x, row)) for c in (0, 2)]

        for n in range(min(AHEAD, len(places))):
            turned(n)
        for n, (x, row) in enumerate(places):
            if n + AHEAD < len(places):
                turned(n + AHEAD)
            rows = pl.ds(row, ROWS)
            hx, hy, hz = (self.load(H, c, x, row) for c in range(3))
            hx_z, hy_z = (self.load(H, c, x, row - 1) for c in (0, 1))
            hy_x, hz_x = (self.load(H, c, x - 1, row) for c in (1, 2))
            hx_y, hz_y = rolled.pop(n)
            for j in range(self.tiles if last else self.tiles + 1):
                ec, eb, bm = (ref[x, j, rows, :] for ref in (self.EC, self.EB, self.BM))
                curls = (
                    (hz[j] - hz_y[j]) - (hy[j] - hy_z[j]),
                    (hx[j] - hx_z[j]) - (hz[j] - hz_x[j]),
                    (hy[j] - hy_x[j]) - (hx[j] - hx_y[j]),
                )
                for c in range(3):
                    e, r = E[c, x, j, rows, :], R[c, x, j, rows, :]
                    u = bm * (e - r)
                    if step > 1:
                        u = KEEP * U[c, x, j, rows, :] + u
                    if not last:
                        U[c, x, j, rows, :] = u
                        R[c, x, j, rows, :] = r + u
                    value = ec * e + eb * (curls[c] - u)
                    if out is None:
                        E[c, x, j, rows, :] = value
                    else:
                        z = (n % len(zsteps)) * ROWS
                        out[c, x - STEPS, z : z + ROWS, j * LANES : (j + 1) * LANES] = value


def groups(begin, end, act, size):
    whole = (end - begin) // size

    def run(n, carry):
        x = begin + n * size
        act(*(x + i for i in range(size)))
        return carry

    if whole > 1:
        lax.fori_loop(0, whole, run, 0)
    elif whole:
        act(*range(begin, begin + size))
    if begin + whole * size < end:
        act(*range(begin + whole * size, end))


def loop(begin, end, act, unroll):
    def run(x, carry):
        act(x)
        return carry

    lax.fori_loop(begin, end, run, 0, unroll=unroll)


def prepare(e_ref, h_ref, p_ref, eps_ref, res_ref, side_ref, *state):
    block = Block(eps_ref.shape, state)
    refs = (e_ref, h_ref, p_ref, eps_ref, res_ref)
    for array in range(ARRAYS):
        src = pick(refs, array)

        def own_plane(x, array=array, src=src):
            for j in range(block.tiles):
                lanes = slice(j * LANES, (j + 1) * LANES)
                for z in range(0, block.zcount, ROWS):
                    block.put(array, x + STEPS, block.own + z, j, src[x, z : z + ROWS, lanes])
                block.put(array, x + STEPS, block.halo, j, side_ref[array, x, :, lanes])

        loop(0, block.xcount, own_plane, 4)
    loop(0, block.extent, block.guards, 1)
    loop(0, block.extent, block.magnetic_coefficients, 2)
    coefficients = functools.partial(block.electric_coefficients, columns=range(block.tiles))
    loop(STEPS, STEPS + block.xcount, coefficients, 2)


def prepare_ends(shape, low_ref, high_ref, *states):
    block = Block(shape, states[len(states) // 2 :])
    per = LANES // SLOT
    for array in range(ARRAYS):
        for x in range(block.xcount):
            block.put_ends(array, x + STEPS, low_ref if x < per else high_ref, x % per)
    coefficients = functools.partial(block.electric_coefficients, columns=(block.tiles,))
    loop(STEPS, STEPS + block.xcount, coefficients, 2)


def groups(begin, end, act, size):
    whole = (end - begin) // size

    def run(n, carry):
        x = begin + n * size
        act(*(x + i for i in range(size)))
        return carry

    if whole > 1:
        lax.fori_loop(0, whole, run, 0)
    elif whole:
        act(*range(begin, begin + size))
    if begin + whole * size < end:
        act(*range(begin + whole * size, end))


def inner(shape, *states):
    block = Block(shape, states[len(states) // 2 :])
    for step in range(1, STEPS + 1):
        last = STEPS + block.xcount - step
        groups(STEPS + step - 1, last, block.magnetic, GROUP)
        groups(STEPS + step, last, functools.partial(block.electric, step=step), GROUP)


def pack_near(first_ref, second_ref, near_ref):
    begin = pl.multiple_of((1 - lax.axis_index("gz")) * (first_ref.shape[1] - ROWS), ROWS)
    near_ref[0] = first_ref[:, pl.ds(begin, ROWS), :]
    near_ref[1] = second_ref[:, pl.ds(begin, ROWS), :]


def arrivals(block, first, second):
    for above, refs in ((even("gx"), first), (jnp.logical_not(even("gx")), second)):
        at = 0
        for array, count in faces():
            for i in range(count):
                plane = jnp.where(above, block.xcount + STEPS + i, STEPS - 1 - i)
                yield array, plane, at + i, STEPS * array + jnp.where(above, i, STEPS - 1 - i), *refs
            at += count


def halo_planes(block):
    return (*range(1, STEPS), *range(STEPS + block.xcount, block.extent - 1))


def place_arrivals(shape, first_ref, second_ref, corner_first_ref, corner_second_ref, *states):
    block = Block(shape, states[len(states) // 2 :])
    per = LANES // SLOT
    came = arrivals(block, (first_ref, corner_first_ref), (second_ref, corner_second_ref))
    for array, plane, at, slot, face, corner in came:
        for j in range(block.tiles):
            for z in range(0, block.zcount, ROWS):
                block.put(array, plane, block.own + z, j, face[at, z : z + ROWS, j * LANES : (j + 1) * LANES])
        block.put_ends(array, plane, corner, lax.rem(slot, per), lax.div(slot, per))
    for plane in halo_planes(block):
        block.electric_coefficients(plane, range(block.tiles), [block.own + z for z in range(0, block.zcount, ROWS)])
        block.electric_coefficients(plane, (block.tiles,))


def outer(shape, near_ref, *rest):
    e_stage, h_stage, sent = rest[-3:]
    count = (len(rest) - 5) // 2
    e_out, h_out = rest[count : count + 2]
    block = Block(shape, rest[count + 2 : -3])
    xcount, zcount = block.xcount, block.zcount
    moves = []

    def send(stage, out, begin, end):
        part = slice(begin - STEPS, end - STEPS)
        move = pltpu.make_async_copy(stage.at[:, part], out.at[:, part], sent.at[len(moves)])
        move.start()
        moves.append(move)

    def stage(ref, into, scale, begin, end):
        for x in range(begin, end):
            for c in range(3):
                for j in range(block.tiles):
                    lanes = slice(j * LANES, (j + 1) * LANES)
                    for z in range(0, zcount, ROWS):
                        value = ref[c, x, j, pl.ds(block.own + z, ROWS), :]
                        into[c, x - STEPS, z : z + ROWS, lanes] = value if scale is None else value * scale

    middle = (2 * STEPS, xcount)
    stage(block.E, e_stage, None, *middle)
    send(e_stage, e_out, *middle)
    stage(block.H, h_stage, 6.0, *middle)
    send(h_stage, h_out, *middle)
    for array, plane, at, _, side in arrivals(block, (near_ref.at[0],), (near_ref.at[1],)):
        for j in range(block.tiles):
            value = side[at, :, j * LANES : (j + 1) * LANES]
            block.put(array, plane, block.halo, j, value)
    for plane in halo_planes(block):
        block.electric_coefficients(plane, range(block.tiles), (block.halo,))
    for step in range(1, STEPS + 1):
        above = xcount + STEPS - step
        block.magnetic(*range(step - 1, step - 1 + STEPS), *range(above, above + STEPS))
        act = functools.partial(block.electric, step=step)
        low, high = range(step, step + STEPS), range(above, above + STEPS)
        if step < STEPS:
            act(*low, *high)
        else:
            for part in (low, high):
                stage(block.H, h_stage, 6.0, part.start, part.stop)
                send(h_stage, h_out, part.start, part.stop)
                act(*part, out=e_stage)
                send(e_stage, e_out, part.start, part.stop)
    for move in moves:
        move.wait()


def call(kernel, outs, args, cost, aliases=None, scratch=(), spec=pltpu.VMEM, hbm=0):
    args = [pltpu.with_memory_space_constraint(a, spec) for a in args]
    work = int(cost * COST)
    return pl.pallas_call(
        kernel,
        out_shape=outs,
        in_specs=[pl.BlockSpec(memory_space=spec)] * len(args),
        out_specs=[pl.BlockSpec(memory_space=pltpu.HBM if i < hbm else pltpu.VMEM) for i in range(len(outs))],
        scratch_shapes=scratch,
        input_output_aliases=aliases or {},
        cost_estimate=pl.CostEstimate(flops=work, bytes_accessed=work, transcendentals=0),
        compiler_params=pltpu.CompilerParams(vmem_limit_bytes=VMEM_LIMIT),
    )(*args)


def swap(value, axis, begin=0):
    pairs = [(i, i + 1) for i in range(begin, lax.axis_size(axis) - 1, 2)]
    return lax.ppermute(value, axis, pairs + [(b, a) for a, b in pairs])


def kept(*shape):
    return pltpu.VMEM(shape, jnp.float32)


def body(e_field, h_field, polar, permittivity, resonance, dispersive):
    xcount, zcount, ycount = shape = permittivity.shape
    marks = jnp.swapaxes(dispersive, 1, 2)
    face = kept(planes_of(faces()), zcount, ycount)
    first, second, side, *fields = call(
        pack_faces,
        [face, face, kept(ARRAYS, xcount, ROWS, ycount)]
        + [kept(*a.shape) for a in (e_field, h_field, polar, permittivity, resonance)],
        (e_field, h_field, polar, permittivity, resonance, marks),
        1,
        scratch=[
            pltpu.VMEM(shape, jnp.float32),
            pltpu.VMEM(marks.shape, marks.dtype),
            pltpu.SemaphoreType.DMA((6,)),
        ],
        spec=pltpu.HBM,
    )
    side = swap(side, "gz")
    second, first = swap(second, "gx", 1), swap(first, "gx")
    fields = (*fields, side)
    strip = kept(ARRAYS, zcount + ROWS, LANES)
    corner = kept(corner_rows(), zcount + ROWS, LANES)
    strips = call(pack_strips, [strip] * 2, fields, 1)
    *strips, fields = lax.optimization_barrier((*strips, fields))
    strip_second, strip_first = swap(strips[1], "gy", 1), swap(strips[0], "gy")
    extent, tiles, rows = xcount + 2 * STEPS, ycount // LANES + 1, zcount + ROWS + 2 * GUARD
    states = [kept(3, extent, tiles, rows, LANES)] * 4
    states += [kept(extent, tiles, rows, LANES)] * 3 + [kept(extent, tiles, ROWS, LANES)] * 2
    count = len(states)
    state = call(prepare, states, fields, 2)
    strip_first, strip_second, state = lax.optimization_barrier((strip_first, strip_second, state))
    low, high, corner_first, corner_second = call(merge_strips, [strip] * 2 + [corner] * 2, (strip_first, strip_second), 0.2)
    corner_second, corner_first = swap(corner_second, "gx", 1), swap(corner_first, "gx")
    ends = functools.partial(prepare_ends, shape)
    state = call(ends, states, (low, high, *state), 0.1, {2 + i: i for i in range(count)})
    same = {i: i for i in range(count)}
    state = call(functools.partial(inner, shape), states, state, 0.1, same)
    first, second, state = lax.optimization_barrier((first, second, state))
    came = (first, second, corner_first, corner_second)
    near = call(pack_near, [kept(2, planes_of(faces()), ROWS, ycount)], (first, second), 0.2)[0]
    near, came, state = lax.optimization_barrier((near, came, state))
    near = swap(near, "gz")
    aliases = {len(came) + i: i for i in range(count)}
    state = call(functools.partial(place_arrivals, shape), states, (*came, *state), 0.1, aliases)
    outs = [jax.ShapeDtypeStruct(e_field.shape, jnp.float32), jax.ShapeDtypeStruct(h_field.shape, jnp.float32)]
    scratch = [pltpu.VMEM(e_field.shape, jnp.float32)] * 2 + [pltpu.SemaphoreType.DMA((6,))]
    aliases = {1 + i: 2 + i for i in range(count)}
    ends = (near, *state)
    return tuple(call(functools.partial(outer, shape), outs + states, ends, 1, aliases, scratch, hbm=2)[:2])


def solution(mesh):
    field, cell = P(None, "gx", "gz", "gy"), P("gx", "gz", "gy")
    return jax.shard_map(
        body,
        mesh=mesh,
        in_specs=(field, field, field, cell, cell, cell),
        out_specs=(field, field),
        check_vma=False,
    )
```

```python
import functools
import jax
import jax.numpy as jnp
from jax import lax
from jax.experimental import pallas as pl
from jax.experimental.pallas import tpu as pltpu
from jax.sharding import PartitionSpec as P

STEPS = 5
AHEAD = 2
GROUP = 8
NPML = 8
DT = 0.5
DAMPING = 0.1
STRENGTH = 3.0
SMAX = 0.8
DENOM = 1.0 + DAMPING * DT / 2.0
KEEP = (1.0 - DAMPING * DT / 2.0) / DENOM

LANES = 128
ROWS = 8
SIDE = 8
SLOT = 2 * SIDE
GUARD = 8
VMEM_LIMIT = 8 * 1024 * 1024

EX, HX, PX, EPS, RES = 0, 3, 6, 9, 10
ARRAYS = 11

COST = 3_000_000


def faces():
    parts = [(EX + c, STEPS) for c in range(3)]
    parts += [(HX + c, STEPS if c > 0 else STEPS - 1) for c in range(3)]
    parts += [(a, STEPS - 1) for a in (PX, PX + 1, PX + 2, EPS, RES)]
    return parts


def planes_of(parts):
    return sum(count for _, count in parts)


def pick(refs, array):
    e_ref, h_ref, p_ref, eps_ref, res_ref = refs
    if array < HX:
        return e_ref.at[array]
    if array < PX:
        return h_ref.at[array - HX]
    if array < EPS:
        return p_ref.at[array - PX]
    return eps_ref if array == EPS else res_ref


def even(axis):
    return lax.axis_index(axis) % 2 == 0


def pack_faces(
    e_hbm, h_hbm, p_hbm, eps_hbm, freq_hbm, mark_hbm,
    first_ref, second_ref, side_ref, e_ref, h_ref, p_ref, eps_ref, res_ref,
    freq_ref, mark_ref, arrived,
):
    xcount, zcount, ycount = eps_ref.shape
    xcount = eps_ref.shape[0]
    pairs = ((mark_hbm, mark_ref), (freq_hbm, freq_ref), (eps_hbm, eps_ref))
    pairs += ((e_hbm, e_ref), (h_hbm, h_ref), (p_hbm, p_ref))
    moves = [pltpu.make_async_copy(src, dst, arrived.at[i]) for i, (src, dst) in enumerate(pairs)]
    for move in moves:
        move.start()
    refs = (e_ref, h_ref, p_ref, eps_ref, res_ref)
    begin = pl.multiple_of((1 - lax.axis_index("gz")) * (zcount - ROWS), ROWS)

    def pack(arrays):
        for up, out_ref in ((even("gx"), first_ref), (jnp.logical_not(even("gx")), second_ref)):
            at = 0
            for array, count in faces():
                for i in range(count if array in arrays else 0):
                    out_ref[at + i] = pick(refs, array)[jnp.where(up, xcount - 1 - i, i)]
                at += count
        for array in arrays:
            side_ref[array] = pick(refs, array)[:, pl.ds(begin, ROWS), :]

    shape = (zcount, zcount)
    diagonal = lax.broadcasted_iota(jnp.int32, shape, 0) == lax.broadcasted_iota(jnp.int32, shape, 1)
    moves[0].wait()
    moves[1].wait()
    for x in range(xcount):
        for j in range(ycount // LANES):
            lanes = slice(j * LANES, (j + 1) * LANES)
            row = jnp.broadcast_to(mark_ref[x, j : j + 1, :].astype(jnp.float32), shape)
            mark = jnp.sum(jnp.where(diagonal, row, 0.0), axis=1, keepdims=True)
            freq = freq_ref[x, :, lanes] * DT
            res_ref[x, :, lanes] = mark * (freq * freq / DENOM)
    moves[2].wait()
    pack((EPS, RES))
    for move, array in zip(moves[3:], (EX, HX, PX)):
        move.wait()
        pack(range(array, array + 3))


def slots():
    lane = lax.broadcasted_iota(jnp.int32, (ROWS, LANES), 1)
    return lane, lane // SLOT, lane % SLOT < SIDE


def turn(value, shift):
    shift = shift % LANES
    return pltpu.roll(value, shift, 1) if shift else value


def pack_strips(e_ref, h_ref, p_ref, eps_ref, res_ref, side_ref, first_ref, second_ref):
    xcount, zcount, ycount = eps_ref.shape
    core = lax.axis_index("gz")
    refs = (e_ref, h_ref, p_ref, eps_ref, res_ref)
    own = pl.multiple_of(core * ROWS, ROWS)
    halo = pl.multiple_of((1 - core) * zcount, ROWS)
    lane, slot, left = slots()
    per = LANES // SLOT
    assert xcount == 2 * per and per >= STEPS
    up = even("gy")
    zs = range(0, zcount + ROWS, ROWS)
    for array in range(ARRAYS):
        src = pick(refs, array)
        packed = [[None, None] for _ in zs]
        for x in range(xcount):
            for n, z in enumerate(zs):
                if z < zcount:
                    first, last = src[x, z : z + ROWS, 0:LANES], src[x, z : z + ROWS, ycount - LANES : ycount]
                else:
                    first, last = side_ref[array, x, :, 0:LANES], side_ref[array, x, :, ycount - LANES : ycount]
                ends = turn(jnp.where(lane < SIDE, first, last), SLOT * (x % per) + SIDE)
                before = packed[n][x // per]
                packed[n][x // per] = ends if before is None else jnp.where(slot == x % per, ends, before)
        for n, z in enumerate(zs):
            p = packed[n]
            rows = pl.ds(own + z, ROWS) if z < zcount else pl.ds(halo, ROWS)
            low = jnp.where(left, turn(p[1], -SIDE), p[0])
            high = jnp.where(left, p[0], turn(p[1], SIDE))
            first_ref[array, rows, :] = jnp.where(up, high, low)
            second_ref[array, rows, :] = jnp.where(up, low, high)


def merge_strips(first_ref, second_ref, low_ref, high_ref, corner_first_ref, corner_second_ref):
    _, slot, left = slots()
    up, over = even("gy"), even("gx")
    per = LANES // SLOT
    for t in range(first_ref.shape[1] // ROWS):
        rows = slice(t * ROWS, (t + 1) * ROWS)
        packed = ([None] * (corner_rows() + 1), [None] * (corner_rows() + 1))
        for array in range(ARRAYS):
            first, second = first_ref[array, rows, :], second_ref[array, rows, :]
            ahead, behind = jnp.where(up, first, second), jnp.where(up, second, first)
            low = jnp.where(left, behind, ahead)
            high = jnp.where(left, turn(behind, -SIDE), turn(ahead, SIDE))
            low_ref[array, rows, :] = low
            high_ref[array, rows, :] = high
            at, place = divmod(STEPS * array, per)
            begin, end = turn(low, SLOT * place), turn(high, SLOT * (place - per + STEPS))
            for into, value in zip(packed, (jnp.where(over, end, begin), jnp.where(over, begin, end))):
                into[at] = value if into[at] is None else jnp.where(slot >= place, value, into[at])
                into[at + 1] = value if place + STEPS > per else None
        for into, out_ref in zip(packed, (corner_first_ref, corner_second_ref)):
            for n in range(corner_rows()):
                out_ref[n, rows, :] = into[n]


def corner_rows():
    return -(-STEPS * ARRAYS // (LANES // SLOT))


def profile(index, total):
    depth = jnp.maximum(NPML - index, 0.0) + jnp.maximum(index - (total - 1 - NPML), 0.0)
    return SMAX * (depth / NPML) ** 3


class Block:
    def __init__(self, shape, state):
        self.xcount, self.zcount, self.ycount = shape
        self.E, self.H, self.R, self.U, self.EC, self.EB, self.BM, self.HC, self.HB = state
        self.tiles = self.ycount // LANES
        self.extent = self.xcount + 2 * STEPS
        self.zsteps = self.zcount // ROWS + 1
        core = lax.axis_index("gz")
        self.own = pl.multiple_of(GUARD + core * ROWS, ROWS)
        self.halo = pl.multiple_of(GUARD + (1 - core) * self.zcount, ROWS)
        self.lane = lax.broadcasted_iota(jnp.int32, (ROWS, LANES), 1)

    def put(self, array, plane, row, j, value):
        rows = pl.ds(row, ROWS)
        if array < HX:
            self.E[array, plane, j, rows, :] = value
        elif array < PX:
            self.H[array - HX, plane, j, rows, :] = value * (1.0 / 6.0)
        elif array < EPS:
            self.R[array - PX, plane, j, rows, :] = value * (1.0 / 3.0)
        elif array == EPS:
            self.EC[plane, j, rows, :] = value
        else:
            self.BM[plane, j, rows, :] = value

    def put_ends(self, array, plane, packed, slot, row=None):
        for t in range(self.zsteps):
            ends = pltpu.roll(packed[array if row is None else row, t * ROWS : (t + 1) * ROWS, :], LANES - SIDE - SLOT * slot, 1)
            self.put(array, plane, GUARD + t * ROWS, self.tiles, ends)

    def place(self, x, j):
        xtotal = self.xcount * lax.axis_size("gx")
        ytotal = self.ycount * lax.axis_size("gy")
        yplace = lax.axis_index("gy") * self.ycount
        xpos = lax.axis_index("gx") * self.xcount + x - STEPS
        lane = self.lane
        inside = jnp.full((ROWS, LANES), (xpos >= 0) & (xpos < xtotal))
        if j < self.tiles:
            ypos = yplace + j * LANES + lane
        else:
            ypos = yplace + jnp.where(lane < SIDE, self.ycount + lane, lane - LANES)
            inside = inside & ((lane < SIDE) | (lane >= LANES - SIDE)) & (ypos >= 0) & (ypos < ytotal)
        xsigma = profile(jnp.full((ROWS, LANES), xpos, jnp.int32).astype(jnp.float32), xtotal)
        return (xsigma + profile(ypos.astype(jnp.float32), ytotal)) * (DT / 2.0), inside

    def magnetic_coefficients(self, x):
        for j in range(self.tiles + 1):
            half, inside = self.place(x, j)
            over = 1.0 / (1.0 + half)
            self.HC[x, j] = jnp.where(inside, (1.0 - half) * over, 0.0)
            self.HB[x, j] = jnp.where(inside, (DT / 6.0) * over, 0.0)

    def electric_coefficients(self, x, columns):
        for j in columns:
            half, inside = self.place(x, j)
            for row in range(GUARD, GUARD + self.zsteps * ROWS, ROWS):
                rows = pl.ds(row, ROWS)
                eps = self.EC[x, j, rows, :]
                over = 1.0 / jnp.where(inside, eps + half, 1.0)
                self.EC[x, j, rows, :] = jnp.where(inside, (eps - half) * over, 0.0)
                self.EB[x, j, rows, :] = jnp.where(inside, (6.0 * DT) * over, 0.0)

    def guards(self, x):
        zero = jnp.zeros((ROWS, LANES), jnp.float32)
        end = GUARD + self.zsteps * ROWS
        for j in range(self.tiles + 1):
            for c in range(3):
                self.H[c, x, j, 0:GUARD, :] = zero
                self.E[c, x, j, end : end + ROWS, :] = zero

    def load(self, ref, c, x, row):
        return [ref[c, x, j, pl.ds(row, ROWS), :] for j in range(self.tiles + 1)]

    def next_lane(self, v):
        r = [turn(t, -1) for t in v]
        return [jnp.where(self.lane == LANES - 1, r[(j + 1) % len(v)], r[j]) for j in range(len(v))]

    def previous_lane(self, v):
        r = [turn(t, 1) for t in v]
        return [jnp.where(self.lane == 0, r[j - 1], r[j]) for j in range(len(v))]

    def magnetic(self, *planes):
        E, H = self.E, self.H
        places = [(x, GUARD + t * ROWS) for x in planes for t in range(self.zsteps)]
        rolled = {}

        def turned(n):
            x, row = places[n]
            rolled[n] = [self.next_lane(self.load(E, c, x, row)) for c in (0, 2)]

        for n in range(min(AHEAD, len(places))):
            turned(n)
        for n, (x, row) in enumerate(places):
            if n + AHEAD < len(places):
                turned(n + AHEAD)
            rows = pl.ds(row, ROWS)
            ex, ey, ez = (self.load(E, c, x, row) for c in range(3))
            ex_z, ey_z = (self.load(E, c, x, row + 1) for c in (0, 1))
            ey_x, ez_x = (self.load(E, c, x + 1, row) for c in (1, 2))
            ex_y, ez_y = rolled.pop(n)
            for j in range(self.tiles + 1):
                hc, hb = self.HC[x, j], self.HB[x, j]
                curls = (
                    (ez_y[j] - ez[j]) - (ey_z[j] - ey[j]),
                    (ex_z[j] - ex[j]) - (ez_x[j] - ez[j]),
                    (ey_x[j] - ey[j]) - (ex_y[j] - ex[j]),
                )
                for c in range(3):
                    H[c, x, j, rows, :] = hc * H[c, x, j, rows, :] - hb * curls[c]

    def electric(self, *planes, step, out=None):
        E, H, R, U = self.E, self.H, self.R, self.U
        last = step == STEPS
        zsteps = range(self.zsteps - 1 if last else self.zsteps)
        places = [(x, self.own + t * ROWS if last else GUARD + t * ROWS) for x in planes for t in zsteps]
        rolled = {}

        def turned(n):
            x, row = places[n]
            rolled[n] = [self.previous_lane(self.load(H, c, x, row)) for c in (0, 2)]

        for n in range(min(AHEAD, len(places))):
            turned(n)
        for n, (x, row) in enumerate(places):
            if n + AHEAD < len(places):
                turned(n + AHEAD)
            rows = pl.ds(row, ROWS)
            hx, hy, hz = (self.load(H, c, x, row) for c in range(3))
            hx_z, hy_z = (self.load(H, c, x, row - 1) for c in (0, 1))
            hy_x, hz_x = (self.load(H, c, x - 1, row) for c in (1, 2))
            hx_y, hz_y = rolled.pop(n)
            for j in range(self.tiles if last else self.tiles + 1):
                ec, eb, bm = (ref[x, j, rows, :] for ref in (self.EC, self.EB, self.BM))
                curls = (
                    (hz[j] - hz_y[j]) - (hy[j] - hy_z[j]),
                    (hx[j] - hx_z[j]) - (hz[j] - hz_x[j]),
                    (hy[j] - hy_x[j]) - (hx[j] - hx_y[j]),
                )
                for c in range(3):
                    e, r = E[c, x, j, rows, :], R[c, x, j, rows, :]
                    u = bm * (e - r)
                    if step > 1:
                        u = KEEP * U[c, x, j, rows, :] + u
                    if not last:
                        U[c, x, j, rows, :] = u
                        R[c, x, j, rows, :] = r + u
                    value = ec * e + eb * (curls[c] - u)
                    if out is None:
                        E[c, x, j, rows, :] = value
                    else:
                        z = (n % len(zsteps)) * ROWS
                        out[c, x - STEPS, z : z + ROWS, j * LANES : (j + 1) * LANES] = value


def groups(begin, end, act, size):
    whole = (end - begin) // size

    def run(n, carry):
        x = begin + n * size
        act(*(x + i for i in range(size)))
        return carry

    if whole > 1:
        lax.fori_loop(0, whole, run, 0)
    elif whole:
        act(*range(begin, begin + size))
    if begin + whole * size < end:
        act(*range(begin + whole * size, end))


def loop(begin, end, act, unroll):
    def run(x, carry):
        act(x)
        return carry

    lax.fori_loop(begin, end, run, 0, unroll=unroll)


def prepare(e_ref, h_ref, p_ref, eps_ref, res_ref, side_ref, *state):
    block = Block(eps_ref.shape, state)
    refs = (e_ref, h_ref, p_ref, eps_ref, res_ref)
    for array in range(ARRAYS):
        src = pick(refs, array)

        def own_plane(x, array=array, src=src):
            for j in range(block.tiles):
                lanes = slice(j * LANES, (j + 1) * LANES)
                for z in range(0, block.zcount, ROWS):
                    block.put(array, x + STEPS, block.own + z, j, src[x, z : z + ROWS, lanes])
                block.put(array, x + STEPS, block.halo, j, side_ref[array, x, :, lanes])

        loop(0, block.xcount, own_plane, 4)
    loop(0, block.extent, block.guards, 1)
    loop(0, block.extent, block.magnetic_coefficients, 2)
    coefficients = functools.partial(block.electric_coefficients, columns=range(block.tiles))
    loop(STEPS, STEPS + block.xcount, coefficients, 2)


def prepare_ends(shape, low_ref, high_ref, *states):
    block = Block(shape, states[len(states) // 2 :])
    per = LANES // SLOT
    for array in range(ARRAYS):
        for x in range(block.xcount):
            block.put_ends(array, x + STEPS, low_ref if x < per else high_ref, x % per)
    coefficients = functools.partial(block.electric_coefficients, columns=(block.tiles,))
    loop(STEPS, STEPS + block.xcount, coefficients, 2)


def groups(begin, end, act, size):
    whole = (end - begin) // size

    def run(n, carry):
        x = begin + n * size
        act(*(x + i for i in range(size)))
        return carry

    if whole > 1:
        lax.fori_loop(0, whole, run, 0)
    elif whole:
        act(*range(begin, begin + size))
    if begin + whole * size < end:
        act(*range(begin + whole * size, end))


def inner(shape, *states):
    block = Block(shape, states[len(states) // 2 :])
    for step in range(1, STEPS + 1):
        last = STEPS + block.xcount - step
        groups(STEPS + step - 1, last, block.magnetic, GROUP)
        groups(STEPS + step, last, functools.partial(block.electric, step=step), GROUP)


NEAR = ROWS - STEPS + 1


def depth(array):
    return STEPS if array < HX + 2 else STEPS - 1


def near_places():
    row, places = NEAR, []
    for face in range(2):
        at = 0
        for array, count in faces():
            for i in range(count):
                places.append((face, at + i, row, depth(array)))
                row += depth(array)
            at += count
    return places, -(-(row + NEAR) // ROWS) * ROWS


def pack_near(first_ref, second_ref, near_ref):
    low_core = lax.axis_index("gz") == 0
    zcount, ycount = first_ref.shape[1:]
    places, rows = near_places()
    near_ref[0:ROWS, :] = jnp.zeros((ROWS, ycount), jnp.float32)
    near_ref[rows - ROWS :, :] = jnp.zeros((ROWS, ycount), jnp.float32)
    for face, at, row, count in places:
        ref = (first_ref, second_ref)[face]
        near_ref[row : row + count, :] = jnp.where(low_core, ref[at, zcount - count :, :], ref[at, 0:count, :])


def arrivals(block, first, second):
    for above, refs in ((even("gx"), first), (jnp.logical_not(even("gx")), second)):
        at = 0
        for array, count in faces():
            for i in range(count):
                plane = jnp.where(above, block.xcount + STEPS + i, STEPS - 1 - i)
                yield array, plane, at + i, STEPS * array + jnp.where(above, i, STEPS - 1 - i), *refs
            at += count


def halo_planes(block):
    return (*range(1, STEPS), *range(STEPS + block.xcount, block.extent - 1))


def outer(shape, first_ref, second_ref, corner_first_ref, corner_second_ref, near_ref, *rest):
    e_stage, h_stage, sent = rest[-3:]
    count = (len(rest) - 5) // 2
    e_out, h_out = rest[count : count + 2]
    block = Block(shape, rest[count + 2 : -3])
    xcount, zcount = block.xcount, block.zcount
    moves = []

    def send(stage, out, begin, end):
        part = slice(begin - STEPS, end - STEPS)
        move = pltpu.make_async_copy(stage.at[:, part], out.at[:, part], sent.at[len(moves)])
        move.start()
        moves.append(move)

    def stage(ref, into, scale, begin, end):
        for x in range(begin, end):
            for c in range(3):
                for j in range(block.tiles):
                    lanes = slice(j * LANES, (j + 1) * LANES)
                    for z in range(0, zcount, ROWS):
                        value = ref[c, x, j, pl.ds(block.own + z, ROWS), :]
                        into[c, x - STEPS, z : z + ROWS, lanes] = value if scale is None else value * scale

    middle = (2 * STEPS, xcount)
    stage(block.E, e_stage, None, *middle)
    send(e_stage, e_out, *middle)
    stage(block.H, h_stage, 6.0, *middle)
    send(h_stage, h_out, *middle)
    core = lax.axis_index("gz")
    per = LANES // SLOT
    rows_at = {(face, at): (row, count) for face, at, row, count in near_places()[0]}
    faces_in = ((first_ref, corner_first_ref, 0), (second_ref, corner_second_ref, 1))
    for array, plane, at, slot, face, corner, side in arrivals(block, *faces_in):
        row, count = rows_at[side, at]
        for j in range(block.tiles):
            lanes = slice(j * LANES, (j + 1) * LANES)
            for z in range(0, zcount, ROWS):
                block.put(array, plane, block.own + z, j, face[at, z : z + ROWS, lanes])
            begin = near_ref[1 - core, row : row + ROWS, lanes]
            end = near_ref[1 - core, row + count - ROWS : row + count, lanes]
            block.put(array, plane, block.halo, j, jnp.where(core == 0, begin, end))
        block.put_ends(array, plane, corner, lax.rem(slot, per), lax.div(slot, per))
    for plane in halo_planes(block):
        block.electric_coefficients(plane, range(block.tiles + 1))
    for step in range(1, STEPS + 1):
        above = xcount + STEPS - step
        block.magnetic(*range(step - 1, step - 1 + STEPS), *range(above, above + STEPS))
        act = functools.partial(block.electric, step=step)
        low, high = range(step, step + STEPS), range(above, above + STEPS)
        if step < STEPS:
            act(*low, *high)
        else:
            for part in (low, high):
                stage(block.H, h_stage, 6.0, part.start, part.stop)
                send(h_stage, h_out, part.start, part.stop)
                act(*part, out=e_stage)
                send(e_stage, e_out, part.start, part.stop)
    for move in moves:
        move.wait()


def call(kernel, outs, args, cost, aliases=None, scratch=(), spec=pltpu.VMEM, hbm=0):
    args = [pltpu.with_memory_space_constraint(a, spec) for a in args]
    work = int(cost * COST)
    return pl.pallas_call(
        kernel,
        out_shape=outs,
        in_specs=[pl.BlockSpec(memory_space=spec)] * len(args),
        out_specs=[pl.BlockSpec(memory_space=pltpu.HBM if i < hbm else pltpu.VMEM) for i in range(len(outs))],
        scratch_shapes=scratch,
        input_output_aliases=aliases or {},
        cost_estimate=pl.CostEstimate(flops=work, bytes_accessed=work, transcendentals=0),
        compiler_params=pltpu.CompilerParams(vmem_limit_bytes=VMEM_LIMIT),
    )(*args)


def swap(value, axis, begin=0):
    pairs = [(i, i + 1) for i in range(begin, lax.axis_size(axis) - 1, 2)]
    return lax.ppermute(value, axis, pairs + [(b, a) for a, b in pairs])


def kept(*shape):
    return pltpu.VMEM(shape, jnp.float32)


def body(e_field, h_field, polar, permittivity, resonance, dispersive):
    xcount, zcount, ycount = shape = permittivity.shape
    marks = jnp.swapaxes(dispersive, 1, 2)
    face = kept(planes_of(faces()), zcount, ycount)
    first, second, side, *fields = call(
        pack_faces,
        [face, face, kept(ARRAYS, xcount, ROWS, ycount)]
        + [kept(*a.shape) for a in (e_field, h_field, polar, permittivity, resonance)],
        (e_field, h_field, polar, permittivity, resonance, marks),
        1,
        scratch=[
            pltpu.VMEM(shape, jnp.float32),
            pltpu.VMEM(marks.shape, marks.dtype),
            pltpu.SemaphoreType.DMA((6,)),
        ],
        spec=pltpu.HBM,
    )
    side = swap(side, "gz")
    second, first = swap(second, "gx", 1), swap(first, "gx")
    fields = (*fields, side)
    strip = kept(ARRAYS, zcount + ROWS, LANES)
    corner = kept(corner_rows(), zcount + ROWS, LANES)
    strips = call(pack_strips, [strip] * 2, fields, 1)
    *strips, fields = lax.optimization_barrier((*strips, fields))
    strip_second, strip_first = swap(strips[1], "gy", 1), swap(strips[0], "gy")
    extent, tiles, rows = xcount + 2 * STEPS, ycount // LANES + 1, zcount + ROWS + 2 * GUARD
    states = [kept(3, extent, tiles, rows, LANES)] * 4
    states += [kept(extent, tiles, rows, LANES)] * 3 + [kept(extent, tiles, ROWS, LANES)] * 2
    count = len(states)
    state = call(prepare, states, fields, 2)
    strip_first, strip_second, state = lax.optimization_barrier((strip_first, strip_second, state))
    low, high, corner_first, corner_second = call(merge_strips, [strip] * 2 + [corner] * 2, (strip_first, strip_second), 0.2)
    corner_second, corner_first = swap(corner_second, "gx", 1), swap(corner_first, "gx")
    ends = functools.partial(prepare_ends, shape)
    state = call(ends, states, (low, high, *state), 0.1, {2 + i: i for i in range(count)})
    same = {i: i for i in range(count)}
    state = call(functools.partial(inner, shape), states, state, 0.1, same)
    first, second, state = lax.optimization_barrier((first, second, state))
    near = call(pack_near, [kept(near_places()[1], ycount)], (first, second), 0.2)[0]
    near = lax.all_gather(near, "gz")
    came = (first, second, corner_first, corner_second, near)
    outs = [jax.ShapeDtypeStruct(e_field.shape, jnp.float32), jax.ShapeDtypeStruct(h_field.shape, jnp.float32)]
    scratch = [pltpu.VMEM(e_field.shape, jnp.float32)] * 2 + [pltpu.SemaphoreType.DMA((6,))]
    aliases = {len(came) + i: 2 + i for i in range(count)}
    ends = (*came, *state)
    return tuple(call(functools.partial(outer, shape), outs + states, ends, 1, aliases, scratch, hbm=2)[:2])


def solution(mesh):
    field, cell = P(None, "gx", "gz", "gy"), P("gx", "gz", "gy")
    return jax.shard_map(
        body,
        mesh=mesh,
        in_specs=(field, field, field, cell, cell, cell),
        out_specs=(field, field),
        check_vma=False,
    )
```

```python
import functools
import jax
import jax.numpy as jnp
from jax import lax
from jax.experimental import pallas as pl
from jax.experimental.pallas import tpu as pltpu
from jax.sharding import PartitionSpec as P

STEPS = 5
AHEAD = 2
GROUP = 8
NPML = 8
DT = 0.5
DAMPING = 0.1
STRENGTH = 3.0
SMAX = 0.8
DENOM = 1.0 + DAMPING * DT / 2.0
KEEP = (1.0 - DAMPING * DT / 2.0) / DENOM

LANES = 128
ROWS = 8
SIDE = 8
SLOT = 2 * SIDE
CORNER = 2 * STEPS
GUARD = 8
VMEM_LIMIT = 8 * 1024 * 1024

EX, HX, PX, EPS, RES = 0, 3, 6, 9, 10
ARRAYS = 11

COST = 3_000_000


def faces():
    parts = [(EX + c, STEPS) for c in range(3)]
    parts += [(HX + c, STEPS if c > 0 else STEPS - 1) for c in range(3)]
    parts += [(a, STEPS - 1) for a in (PX, PX + 1, PX + 2, EPS, RES)]
    return parts


def planes_of(parts):
    return sum(count for _, count in parts)


def pick(refs, array):
    e_ref, h_ref, p_ref, eps_ref, res_ref = refs
    if array < HX:
        return e_ref.at[array]
    if array < PX:
        return h_ref.at[array - HX]
    if array < EPS:
        return p_ref.at[array - PX]
    return eps_ref if array == EPS else res_ref


def even(axis):
    return lax.axis_index(axis) % 2 == 0


def pack_faces(
    e_hbm, h_hbm, p_hbm, eps_hbm, freq_hbm, mark_hbm,
    first_ref, second_ref, side_ref, e_ref, h_ref, p_ref, eps_ref, res_ref,
    freq_ref, mark_ref, arrived,
):
    xcount, zcount, ycount = eps_ref.shape
    xcount = eps_ref.shape[0]
    pairs = ((mark_hbm, mark_ref), (freq_hbm, freq_ref), (eps_hbm, eps_ref))
    pairs += ((e_hbm, e_ref), (h_hbm, h_ref), (p_hbm, p_ref))
    moves = [pltpu.make_async_copy(src, dst, arrived.at[i]) for i, (src, dst) in enumerate(pairs)]
    for move in moves:
        move.start()
    refs = (e_ref, h_ref, p_ref, eps_ref, res_ref)
    begin = pl.multiple_of((1 - lax.axis_index("gz")) * (zcount - ROWS), ROWS)

    def pack(arrays):
        for up, out_ref in ((even("gx"), first_ref), (jnp.logical_not(even("gx")), second_ref)):
            at = 0
            for array, count in faces():
                for i in range(count if array in arrays else 0):
                    out_ref[at + i] = pick(refs, array)[jnp.where(up, xcount - 1 - i, i)]
                at += count
        for array in arrays:
            side_ref[array] = pick(refs, array)[:, pl.ds(begin, ROWS), :]

    shape = (zcount, zcount)
    diagonal = lax.broadcasted_iota(jnp.int32, shape, 0) == lax.broadcasted_iota(jnp.int32, shape, 1)
    moves[0].wait()
    moves[1].wait()
    for x in range(xcount):
        for j in range(ycount // LANES):
            lanes = slice(j * LANES, (j + 1) * LANES)
            row = jnp.broadcast_to(mark_ref[x, j : j + 1, :].astype(jnp.float32), shape)
            mark = jnp.sum(jnp.where(diagonal, row, 0.0), axis=1, keepdims=True)
            freq = freq_ref[x, :, lanes] * DT
            res_ref[x, :, lanes] = mark * (freq * freq / DENOM)
    moves[2].wait()
    pack((EPS, RES))
    for move, array in zip(moves[3:], (EX, HX, PX)):
        move.wait()
        pack(range(array, array + 3))


def slots():
    lane = lax.broadcasted_iota(jnp.int32, (ROWS, LANES), 1)
    return lane, lane // SLOT, lane % SLOT < SIDE


def turn(value, shift):
    shift = shift % LANES
    return pltpu.roll(value, shift, 1) if shift else value


def pack_strips(e_ref, h_ref, p_ref, eps_ref, res_ref, side_ref, first_ref, second_ref):
    xcount, zcount, ycount = eps_ref.shape
    core = lax.axis_index("gz")
    refs = (e_ref, h_ref, p_ref, eps_ref, res_ref)
    own = pl.multiple_of(core * ROWS, ROWS)
    halo = pl.multiple_of((1 - core) * zcount, ROWS)
    lane, slot, left = slots()
    per = LANES // SLOT
    assert xcount == 2 * per and per >= STEPS
    up = even("gy")
    zs = range(0, zcount + ROWS, ROWS)
    for array in range(ARRAYS):
        src = pick(refs, array)
        packed = [[None, None] for _ in zs]
        for x in range(xcount):
            for n, z in enumerate(zs):
                if z < zcount:
                    first, last = src[x, z : z + ROWS, 0:LANES], src[x, z : z + ROWS, ycount - LANES : ycount]
                else:
                    first, last = side_ref[array, x, :, 0:LANES], side_ref[array, x, :, ycount - LANES : ycount]
                ends = turn(jnp.where(lane < SIDE, first, last), SLOT * (x % per) + SIDE)
                before = packed[n][x // per]
                packed[n][x // per] = ends if before is None else jnp.where(slot == x % per, ends, before)
        for n, z in enumerate(zs):
            p = packed[n]
            rows = pl.ds(own + z, ROWS) if z < zcount else pl.ds(halo, ROWS)
            low = jnp.where(left, turn(p[1], -SIDE), p[0])
            high = jnp.where(left, p[0], turn(p[1], SIDE))
            first_ref[array, rows, :] = jnp.where(up, high, low)
            second_ref[array, rows, :] = jnp.where(up, low, high)


def merge_strips(first_ref, second_ref, low_ref, high_ref, corner_first_ref, corner_second_ref):
    lane, _, left = slots()
    up, over = even("gy"), even("gx")
    per = LANES // SLOT
    for t in range(first_ref.shape[1] // ROWS):
        rows = slice(t * ROWS, (t + 1) * ROWS)
        packed = ([None] * corner_rows(), [None] * corner_rows())
        for array in range(ARRAYS):
            first, second = first_ref[array, rows, :], second_ref[array, rows, :]
            ahead, behind = jnp.where(up, first, second), jnp.where(up, second, first)
            low = jnp.where(left, behind, ahead)
            high = jnp.where(left, turn(behind, -SIDE), turn(ahead, SIDE))
            low_ref[array, rows, :] = low
            high_ref[array, rows, :] = high
            for i in range(STEPS):
                at, place = divmod(STEPS * array + i, LANES // CORNER)
                here = (lane >= CORNER * place) & (lane < CORNER * (place + 1))
                shift = CORNER * place - (SIDE - STEPS)
                begin, end = turn(low, shift - SLOT * i), turn(high, shift - SLOT * (i + per - STEPS))
                for into, value in zip(packed, (jnp.where(over, end, begin), jnp.where(over, begin, end))):
                    into[at] = value if into[at] is None else jnp.where(here, value, into[at])
        for into, out_ref in zip(packed, (corner_first_ref, corner_second_ref)):
            for n in range(corner_rows()):
                out_ref[n, rows, :] = into[n]


def corner_rows():
    return -(-STEPS * ARRAYS // (LANES // CORNER))


def profile(index, total):
    depth = jnp.maximum(NPML - index, 0.0) + jnp.maximum(index - (total - 1 - NPML), 0.0)
    return SMAX * (depth / NPML) ** 3


class Block:
    def __init__(self, shape, state):
        self.xcount, self.zcount, self.ycount = shape
        self.E, self.H, self.R, self.U, self.EC, self.EB, self.BM, self.HC, self.HB = state
        self.tiles = self.ycount // LANES
        self.extent = self.xcount + 2 * STEPS
        self.zsteps = self.zcount // ROWS + 1
        core = lax.axis_index("gz")
        self.own = pl.multiple_of(GUARD + core * ROWS, ROWS)
        self.halo = pl.multiple_of(GUARD + (1 - core) * self.zcount, ROWS)
        self.lane = lax.broadcasted_iota(jnp.int32, (ROWS, LANES), 1)

    def put(self, array, plane, row, j, value):
        rows = pl.ds(row, ROWS)
        if array < HX:
            self.E[array, plane, j, rows, :] = value
        elif array < PX:
            self.H[array - HX, plane, j, rows, :] = value * (1.0 / 6.0)
        elif array < EPS:
            self.R[array - PX, plane, j, rows, :] = value * (1.0 / 3.0)
        elif array == EPS:
            self.EC[plane, j, rows, :] = value
        else:
            self.BM[plane, j, rows, :] = value

    def put_ends(self, array, plane, packed, shift, row=None):
        for t in range(self.zsteps):
            ends = pltpu.roll(packed[array if row is None else row, t * ROWS : (t + 1) * ROWS, :], shift, 1)
            self.put(array, plane, GUARD + t * ROWS, self.tiles, ends)

    def place(self, x, j):
        xtotal = self.xcount * lax.axis_size("gx")
        ytotal = self.ycount * lax.axis_size("gy")
        yplace = lax.axis_index("gy") * self.ycount
        xpos = lax.axis_index("gx") * self.xcount + x - STEPS
        lane = self.lane
        inside = jnp.full((ROWS, LANES), (xpos >= 0) & (xpos < xtotal))
        if j < self.tiles:
            ypos = yplace + j * LANES + lane
        else:
            ypos = yplace + jnp.where(lane < SIDE, self.ycount + lane, lane - LANES)
            inside = inside & ((lane < SIDE) | (lane >= LANES - SIDE)) & (ypos >= 0) & (ypos < ytotal)
        xsigma = profile(jnp.full((ROWS, LANES), xpos, jnp.int32).astype(jnp.float32), xtotal)
        return (xsigma + profile(ypos.astype(jnp.float32), ytotal)) * (DT / 2.0), inside

    def magnetic_coefficients(self, x):
        for j in range(self.tiles + 1):
            half, inside = self.place(x, j)
            over = 1.0 / (1.0 + half)
            self.HC[x, j] = jnp.where(inside, (1.0 - half) * over, 0.0)
            self.HB[x, j] = jnp.where(inside, (DT / 6.0) * over, 0.0)

    def electric_coefficients(self, x, columns, at=None):
        for j in columns:
            half, inside = self.place(x, j)
            for row in at or range(GUARD, GUARD + self.zsteps * ROWS, ROWS):
                rows = pl.ds(row, ROWS)
                eps = self.EC[x, j, rows, :]
                over = 1.0 / jnp.where(inside, eps + half, 1.0)
                self.EC[x, j, rows, :] = jnp.where(inside, (eps - half) * over, 0.0)
                self.EB[x, j, rows, :] = jnp.where(inside, (6.0 * DT) * over, 0.0)

    def guards(self, x):
        zero = jnp.zeros((ROWS, LANES), jnp.float32)
        end = GUARD + self.zsteps * ROWS
        for j in range(self.tiles + 1):
            for c in range(3):
                self.H[c, x, j, 0:GUARD, :] = zero
                self.E[c, x, j, end : end + ROWS, :] = zero

    def load(self, ref, c, x, row):
        return [ref[c, x, j, pl.ds(row, ROWS), :] for j in range(self.tiles + 1)]

    def next_lane(self, v):
        r = [turn(t, -1) for t in v]
        return [jnp.where(self.lane == LANES - 1, r[(j + 1) % len(v)], r[j]) for j in range(len(v))]

    def previous_lane(self, v):
        r = [turn(t, 1) for t in v]
        return [jnp.where(self.lane == 0, r[j - 1], r[j]) for j in range(len(v))]

    def magnetic(self, *planes):
        E, H = self.E, self.H
        places = [(x, GUARD + t * ROWS) for x in planes for t in range(self.zsteps)]
        rolled = {}

        def turned(n):
            x, row = places[n]
            rolled[n] = [self.next_lane(self.load(E, c, x, row)) for c in (0, 2)]

        for n in range(min(AHEAD, len(places))):
            turned(n)
        for n, (x, row) in enumerate(places):
            if n + AHEAD < len(places):
                turned(n + AHEAD)
            rows = pl.ds(row, ROWS)
            ex, ey, ez = (self.load(E, c, x, row) for c in range(3))
            ex_z, ey_z = (self.load(E, c, x, row + 1) for c in (0, 1))
            ey_x, ez_x = (self.load(E, c, x + 1, row) for c in (1, 2))
            ex_y, ez_y = rolled.pop(n)
            for j in range(self.tiles + 1):
                hc, hb = self.HC[x, j], self.HB[x, j]
                curls = (
                    (ez_y[j] - ez[j]) - (ey_z[j] - ey[j]),
                    (ex_z[j] - ex[j]) - (ez_x[j] - ez[j]),
                    (ey_x[j] - ey[j]) - (ex_y[j] - ex[j]),
                )
                for c in range(3):
                    H[c, x, j, rows, :] = hc * H[c, x, j, rows, :] - hb * curls[c]

    def electric(self, *planes, step, out=None):
        E, H, R, U = self.E, self.H, self.R, self.U
        last = step == STEPS
        zsteps = range(self.zsteps - 1 if last else self.zsteps)
        places = [(x, self.own + t * ROWS if last else GUARD + t * ROWS) for x in planes for t in zsteps]
        rolled = {}

        def turned(n):
            x, row = places[n]
            rolled[n] = [self.previous_lane(self.load(H, c, x, row)) for c in (0, 2)]

        for n in range(min(AHEAD, len(places))):
            turned(n)
        for n, (x, row) in enumerate(places):
            if n + AHEAD < len(places):
                turned(n + AHEAD)
            rows = pl.ds(row, ROWS)
            hx, hy, hz = (self.load(H, c, x, row) for c in range(3))
            hx_z, hy_z = (self.load(H, c, x, row - 1) for c in (0, 1))
            hy_x, hz_x = (self.load(H, c, x - 1, row) for c in (1, 2))
            hx_y, hz_y = rolled.pop(n)
            for j in range(self.tiles if last else self.tiles + 1):
                ec, eb, bm = (ref[x, j, rows, :] for ref in (self.EC, self.EB, self.BM))
                curls = (
                    (hz[j] - hz_y[j]) - (hy[j] - hy_z[j]),
                    (hx[j] - hx_z[j]) - (hz[j] - hz_x[j]),
                    (hy[j] - hy_x[j]) - (hx[j] - hx_y[j]),
                )
                for c in range(3):
                    e, r = E[c, x, j, rows, :], R[c, x, j, rows, :]
                    u = bm * (e - r)
                    if step > 1:
                        u = KEEP * U[c, x, j, rows, :] + u
                    if not last:
                        U[c, x, j, rows, :] = u
                        R[c, x, j, rows, :] = r + u
                    value = ec * e + eb * (curls[c] - u)
                    if out is None:
                        E[c, x, j, rows, :] = value
                    else:
                        z = (n % len(zsteps)) * ROWS
                        out[c, x - STEPS, z : z + ROWS, j * LANES : (j + 1) * LANES] = value


def groups(begin, end, act, size):
    whole = (end - begin) // size

    def run(n, carry):
        x = begin + n * size
        act(*(x + i for i in range(size)))
        return carry

    if whole > 1:
        lax.fori_loop(0, whole, run, 0)
    elif whole:
        act(*range(begin, begin + size))
    if begin + whole * size < end:
        act(*range(begin + whole * size, end))


def loop(begin, end, act, unroll):
    def run(x, carry):
        act(x)
        return carry

    lax.fori_loop(begin, end, run, 0, unroll=unroll)


def prepare(e_ref, h_ref, p_ref, eps_ref, res_ref, side_ref, *state):
    block = Block(eps_ref.shape, state)
    refs = (e_ref, h_ref, p_ref, eps_ref, res_ref)
    for array in range(ARRAYS):
        src = pick(refs, array)

        def own_plane(x, array=array, src=src):
            for j in range(block.tiles):
                lanes = slice(j * LANES, (j + 1) * LANES)
                for z in range(0, block.zcount, ROWS):
                    block.put(array, x + STEPS, block.own + z, j, src[x, z : z + ROWS, lanes])
                block.put(array, x + STEPS, block.halo, j, side_ref[array, x, :, lanes])

        loop(0, block.xcount, own_plane, 4)
    loop(0, block.extent, block.guards, 1)
    loop(0, block.extent, block.magnetic_coefficients, 2)
    coefficients = functools.partial(block.electric_coefficients, columns=range(block.tiles))
    loop(STEPS, STEPS + block.xcount, coefficients, 2)


def prepare_ends(shape, low_ref, high_ref, *states):
    block = Block(shape, states[len(states) // 2 :])
    per = LANES // SLOT
    for array in range(ARRAYS):
        for x in range(block.xcount):
            block.put_ends(array, x + STEPS, low_ref if x < per else high_ref, LANES - SIDE - SLOT * (x % per))
    coefficients = functools.partial(block.electric_coefficients, columns=(block.tiles,))
    loop(STEPS, STEPS + block.xcount, coefficients, 2)


def groups(begin, end, act, size):
    whole = (end - begin) // size

    def run(n, carry):
        x = begin + n * size
        act(*(x + i for i in range(size)))
        return carry

    if whole > 1:
        lax.fori_loop(0, whole, run, 0)
    elif whole:
        act(*range(begin, begin + size))
    if begin + whole * size < end:
        act(*range(begin + whole * size, end))


def inner(shape, begin, end, *states):
    block = Block(shape, states[len(states) // 2 :])
    for step in range(begin, end):
        last = STEPS + block.xcount - step
        groups(STEPS + step - 1, last, block.magnetic, GROUP)
        groups(STEPS + step, last, functools.partial(block.electric, step=step), GROUP)


NEAR = ROWS - STEPS + 1


def depth(array):
    return STEPS if array < HX + 2 else STEPS - 1


def near_places():
    row, places = NEAR, []
    for face in range(2):
        at = 0
        for array, count in faces():
            for i in range(count):
                places.append((face, at + i, row, depth(array)))
                row += depth(array)
            at += count
    return places, -(-(row + NEAR) // ROWS) * ROWS


def pack_near(first_ref, second_ref, near_ref):
    low_core = lax.axis_index("gz") == 0
    zcount, ycount = first_ref.shape[1:]
    places, rows = near_places()
    near_ref[0:ROWS, :] = jnp.zeros((ROWS, ycount), jnp.float32)
    near_ref[rows - ROWS :, :] = jnp.zeros((ROWS, ycount), jnp.float32)
    for face, at, row, count in places:
        ref = (first_ref, second_ref)[face]
        near_ref[row : row + count, :] = jnp.where(low_core, ref[at, zcount - count :, :], ref[at, 0:count, :])


def arrivals(block, first, second):
    for above, refs in ((even("gx"), first), (jnp.logical_not(even("gx")), second)):
        at = 0
        for array, count in faces():
            for i in range(count):
                plane = jnp.where(above, block.xcount + STEPS + i, STEPS - 1 - i)
                yield array, plane, at + i, STEPS * array + jnp.where(above, i, STEPS - 1 - i), *refs
            at += count


def halo_planes(block):
    return (*range(1, STEPS), *range(STEPS + block.xcount, block.extent - 1))


def place_arrivals(shape, first_ref, second_ref, corner_first_ref, corner_second_ref, *states):
    block = Block(shape, states[len(states) // 2 :])
    per = LANES // CORNER
    came = arrivals(block, (first_ref, corner_first_ref), (second_ref, corner_second_ref))
    for array, plane, at, slot, face, corner in came:
        for j in range(block.tiles):
            for z in range(0, block.zcount, ROWS):
                block.put(array, plane, block.own + z, j, face[at, z : z + ROWS, j * LANES : (j + 1) * LANES])
        block.put_ends(array, plane, corner, LANES - STEPS - CORNER * lax.rem(slot, per), lax.div(slot, per))
    for plane in halo_planes(block):
        block.electric_coefficients(plane, range(block.tiles), [block.own + z for z in range(0, block.zcount, ROWS)])
        block.electric_coefficients(plane, (block.tiles,))


def outer(shape, near_ref, *rest):
    e_stage, h_stage, sent = rest[-3:]
    count = (len(rest) - 5) // 2
    e_out, h_out = rest[count : count + 2]
    block = Block(shape, rest[count + 2 : -3])
    xcount, zcount = block.xcount, block.zcount
    moves = []

    def send(stage, out, begin, end):
        part = slice(begin - STEPS, end - STEPS)
        move = pltpu.make_async_copy(stage.at[:, part], out.at[:, part], sent.at[len(moves)])
        move.start()
        moves.append(move)

    def stage(ref, into, scale, begin, end):
        for x in range(begin, end):
            for c in range(3):
                for j in range(block.tiles):
                    lanes = slice(j * LANES, (j + 1) * LANES)
                    for z in range(0, zcount, ROWS):
                        value = ref[c, x, j, pl.ds(block.own + z, ROWS), :]
                        into[c, x - STEPS, z : z + ROWS, lanes] = value if scale is None else value * scale

    middle = (2 * STEPS, xcount)
    stage(block.E, e_stage, None, *middle)
    send(e_stage, e_out, *middle)
    stage(block.H, h_stage, 6.0, *middle)
    send(h_stage, h_out, *middle)
    low_core = lax.axis_index("gz") == 0
    rows_at = {(face, at): (row, count) for face, at, row, count in near_places()[0]}
    for array, plane, at, _, face in arrivals(block, (0,), (1,)):
        row, count = rows_at[face, at]
        for j in range(block.tiles):
            lanes = slice(j * LANES, (j + 1) * LANES)
            begin, end = near_ref[row : row + ROWS, lanes], near_ref[row + count - ROWS : row + count, lanes]
            block.put(array, plane, block.halo, j, jnp.where(low_core, begin, end))
    for plane in halo_planes(block):
        block.electric_coefficients(plane, range(block.tiles), (block.halo,))
    for step in range(1, STEPS + 1):
        above = xcount + STEPS - step
        block.magnetic(*range(step - 1, step - 1 + STEPS), *range(above, above + STEPS))
        act = functools.partial(block.electric, step=step)
        low, high = range(step, step + STEPS), range(above, above + STEPS)
        if step < STEPS:
            act(*low, *high)
        else:
            for part in (low, high):
                stage(block.H, h_stage, 6.0, part.start, part.stop)
                send(h_stage, h_out, part.start, part.stop)
                act(*part, out=e_stage)
                send(e_stage, e_out, part.start, part.stop)
    for move in moves:
        move.wait()


def call(kernel, outs, args, cost, aliases=None, scratch=(), spec=pltpu.VMEM, hbm=0):
    args = [pltpu.with_memory_space_constraint(a, spec) for a in args]
    work = int(cost * COST)
    return pl.pallas_call(
        kernel,
        out_shape=outs,
        in_specs=[pl.BlockSpec(memory_space=spec)] * len(args),
        out_specs=[pl.BlockSpec(memory_space=pltpu.HBM if i < hbm else pltpu.VMEM) for i in range(len(outs))],
        scratch_shapes=scratch,
        input_output_aliases=aliases or {},
        cost_estimate=pl.CostEstimate(flops=work, bytes_accessed=work, transcendentals=0),
        compiler_params=pltpu.CompilerParams(vmem_limit_bytes=VMEM_LIMIT),
    )(*args)


def swap(value, axis, begin=0):
    pairs = [(i, i + 1) for i in range(begin, lax.axis_size(axis) - 1, 2)]
    return lax.ppermute(value, axis, pairs + [(b, a) for a, b in pairs])


def kept(*shape):
    return pltpu.VMEM(shape, jnp.float32)


def body(e_field, h_field, polar, permittivity, resonance, dispersive):
    xcount, zcount, ycount = shape = permittivity.shape
    marks = jnp.swapaxes(dispersive, 1, 2)
    face = kept(planes_of(faces()), zcount, ycount)
    first, second, side, *fields = call(
        pack_faces,
        [face, face, kept(ARRAYS, xcount, ROWS, ycount)]
        + [kept(*a.shape) for a in (e_field, h_field, polar, permittivity, resonance)],
        (e_field, h_field, polar, permittivity, resonance, marks),
        1,
        scratch=[
            pltpu.VMEM(shape, jnp.float32),
            pltpu.VMEM(marks.shape, marks.dtype),
            pltpu.SemaphoreType.DMA((6,)),
        ],
        spec=pltpu.HBM,
    )
    side = swap(side, "gz")
    second, first = swap(second, "gx", 1), swap(first, "gx")
    fields = (*fields, side)
    strip = kept(ARRAYS, zcount + ROWS, LANES)
    corner = kept(corner_rows(), zcount + ROWS, LANES)
    strips = call(pack_strips, [strip] * 2, fields, 1)
    *strips, fields = lax.optimization_barrier((*strips, fields))
    strip_second, strip_first = swap(strips[1], "gy", 1), swap(strips[0], "gy")
    extent, tiles, rows = xcount + 2 * STEPS, ycount // LANES + 1, zcount + ROWS + 2 * GUARD
    states = [kept(3, extent, tiles, rows, LANES)] * 4
    states += [kept(extent, tiles, rows, LANES)] * 3 + [kept(extent, tiles, ROWS, LANES)] * 2
    count = len(states)
    state = call(prepare, states, fields, 2)
    strip_first, strip_second, state = lax.optimization_barrier((strip_first, strip_second, state))
    low, high, corner_first, corner_second = call(merge_strips, [strip] * 2 + [corner] * 2, (strip_first, strip_second), 0.2)
    corner_second, corner_first = swap(corner_second, "gx", 1), swap(corner_first, "gx")
    ends = functools.partial(prepare_ends, shape)
    state = call(ends, states, (low, high, *state), 0.1, {2 + i: i for i in range(count)})
    same = {i: i for i in range(count)}
    state = call(functools.partial(inner, shape, 1, STEPS), states, state, 0.1, same)
    first, second, state = lax.optimization_barrier((first, second, state))
    came = (first, second, corner_first, corner_second)
    near = call(pack_near, [kept(near_places()[1], ycount)], (first, second), 0.2)[0]
    near, came, state = lax.optimization_barrier((near, came, state))
    near = swap(near, "gz")
    aliases = {len(came) + i: i for i in range(count)}
    state = call(functools.partial(place_arrivals, shape), states, (*came, *state), 0.1, aliases)
    state = call(functools.partial(inner, shape, STEPS, STEPS + 1), states, state, 0.1, same)
    outs = [jax.ShapeDtypeStruct(e_field.shape, jnp.float32), jax.ShapeDtypeStruct(h_field.shape, jnp.float32)]
    scratch = [pltpu.VMEM(e_field.shape, jnp.float32)] * 2 + [pltpu.SemaphoreType.DMA((6,))]
    aliases = {1 + i: 2 + i for i in range(count)}
    ends = (near, *state)
    return tuple(call(functools.partial(outer, shape), outs + states, ends, 1, aliases, scratch, hbm=2)[:2])


def solution(mesh):
    field, cell = P(None, "gx", "gz", "gy"), P("gx", "gz", "gy")
    return jax.shard_map(
        body,
        mesh=mesh,
        in_specs=(field, field, field, cell, cell, cell),
        out_specs=(field, field),
        check_vma=False,
    )
```
